128 devices in a mesh: ctx: 16 (over y, z), kvh: 8 (over x, core).
Axes of the slice: x: 4, y: 4, z: 4, core: 2. Of those that a mesh axis runs over, the one named last changes fastest.
Arguments:
- query: bfloat16 [4, 4, 16384], P(None, None, 'kvh'), may hold values from -100 to 100
- new_kv: bfloat16 [2, 4, 4, 1024], P(None, None, None, 'kvh'), may hold values from -10 to 10
- kv_cache: bfloat16 [2, 4, 8, 16384, 128], P(None, None, 'kvh', 'ctx'), may hold values from -4 to 4
- lengths: int32 [4], replicated, may hold values from 2 to 16384, as said below
- residual: bfloat16 [4, 4, 16384], P(None, None, ('ctx', 'kvh')), may hold values from -6 to 6
- out_weight: bfloat16 [16384, 16384], P('kvh', 'ctx'), may hold values from -0.75 to 0.75
- norm_gain: float32 [16384], P(('ctx', 'kvh')), may hold values from 0.25 to 1.75
- gate_weight: bfloat16 [26624, 16384], P(('ctx', 'kvh')), may hold values from -0.046875 to 0.046875
- up_weight: bfloat16 [26624, 16384], P(('ctx', 'kvh')), may hold values from -0.046875 to 0.046875
- down_weight: bfloat16 [26624, 16384], P(('ctx', 'kvh')), may hold values from -0.125 to 0.125
Outputs:
- layer_out: bfloat16 [4, 4, 16384], P(None, None, ('ctx', 'kvh'))
The draws below stay inside these ranges and needn't reach their ends.
Inputs may be any that keep to these rules, and one draw needn't show every extreme that they name: `lengths`: at least one sequence has exactly 16384 filled positions.
All inputs are finite; a program needn't handle non-finite values.
Results may differ from the reference program's by a relative error of at most 0.013.
Values may be sent and summed in bfloat16 or wider, within the bound.
A program may use at most 128 MiB of HBM per device.

```python
import math
import jax
import jax.numpy as jnp
from jax import lax

D = 16384
H = 128
KVH = 8
HD = 128
FF = 26624
STEPS = 4
BATCH = 4
CACHE = 16384


def shared_keys(key):
    base = jax.random.normal(key, (BATCH, KVH, CACHE, HD), jnp.float32)
    return jnp.clip(base, -4.0, 4.0)


def draw_query(key, part):
    key = jax.random.fold_in(key, 11)
    shape = (STEPS, BATCH, KVH, H // KVH, HD)
    values = jnp.clip(jax.random.normal(key, shape, jnp.float32), -4.0, 4.0)
    return values.reshape(STEPS, BATCH, H * HD).astype(jnp.bfloat16)


def draw_kv_cache(key, part):
    cached = shared_keys(key)
    key = jax.random.fold_in(key, 12)
    shape = (BATCH, KVH, CACHE, HD)
    values = jnp.clip(jax.random.normal(key, shape, jnp.float32), -4.0, 4.0)
    return jnp.stack([cached, values]).astype(jnp.bfloat16)


def draw_lengths(key, part):
    key = jax.random.fold_in(key, 13)
    first_key, second_key = jax.random.split(key)
    filled = jax.random.randint(first_key, (BATCH,), 2, CACHE + 1, jnp.int32)
    longest = jax.random.randint(second_key, (), 0, BATCH, jnp.int32)
    return jnp.where(jnp.arange(BATCH) == longest, CACHE, filled).astype(jnp.int32)


def strengthened(array, key, source, target, blocks, factor):
    owner, partner = [(jnp.arange(array.shape[axis_at]) // (array.shape[axis_at] // blocks)).reshape([-1 if axis == axis_at else 1 for axis in range(array.ndim)]) for axis_at in (source, target)]
    chosen = jax.random.permutation(key, blocks)[partner]
    strong = (owner == chosen) | (owner == (partner + blocks // 2) % blocks)
    return jnp.where(strong, factor * array, array)


def levels(own_key, dims, shards, least, top_value):
    def one(axis_at, parts):
        draws = jax.random.uniform(jax.random.fold_in(jax.random.fold_in(own_key, 6), axis_at), (parts,), jnp.float32, least / len(shards), top_value / len(shards))
        return jnp.repeat(jnp.exp(draws), dims[axis_at] // parts).reshape((-1,) + (1,) * (len(dims) - axis_at - 1))

    gain = one(*shards[0])
    for cut in shards[1:]:
        gain = gain * one(*cut)
    return gain


def centred(stream_key, dims, deviation, bound, shards=(), kind=jnp.bfloat16):
    array = jax.random.normal(stream_key, dims, jnp.float32) * deviation
    if len(shards) > 0:
        array = levels(stream_key, dims, shards, -0.22, 0.18) * array
    return jnp.clip(array, min=-bound, max=bound).astype(kind)


def heavy_noise(key, dims, scale, bound, cuts, heavy, kind=jnp.bfloat16):
    values = scale * jax.random.normal(key, dims, jnp.float32)
    if cuts:
        values = values * levels(key, dims, cuts, -0.22, 0.18)
    return jnp.clip(strengthened(values, jax.random.fold_in(key, 3), *heavy), -bound, bound).astype(kind)


def setup_inputs(seed: int = 0) -> dict:
    seeds = jax.random.split(jax.random.key(seed), 11)
    return {
        "query": draw_query(jax.random.fold_in(seeds[10], 71), 0),
        "new_kv": centred(seeds[1], (2, STEPS, BATCH, KVH * HD), 2.0, 10.0, ((3, 8),)),
        "kv_cache": draw_kv_cache(jax.random.fold_in(seeds[10], 71), 0),
        "lengths": draw_lengths(jax.random.fold_in(seeds[10], 71), 0),
        "residual": centred(seeds[4], (STEPS, BATCH, D), 1.0, 6.0, ((2, 128),)),
        "out_weight": heavy_noise(seeds[5], (H * HD, D), HD ** -0.5, 0.75, ((0, 8), (1, 16)), (0, 1, 16, 2.0)),
        "norm_gain": jnp.clip(1.0 + 0.15 * jax.random.normal(seeds[6], (D,), jnp.float32), 0.25, 1.75),
        "gate_weight": centred(seeds[7], (FF, D), D ** -0.5, 0.046875, ((0, 128),)),
        "up_weight": centred(seeds[8], (FF, D), D ** -0.5, 0.046875, ((0, 128),)),
        "down_weight": heavy_noise(seeds[9], (FF, D), FF ** -0.5, 0.125, ((0, 128),), (0, 1, 128, 5.5)),
    }


def reference(query, new_kv, kv_cache, lengths, residual, out_weight, norm_gain, gate_weight, up_weight, down_weight):
    per_group = H // KVH
    scale = 1.0 / math.sqrt(HD)
    queries = query.astype(jnp.float32).reshape(STEPS, BATCH, KVH, per_group, HD)
    draft_keys = jnp.transpose(new_kv[0].reshape(STEPS, BATCH, KVH, HD), (1, 2, 0, 3))
    draft_values = jnp.transpose(new_kv[1].reshape(STEPS, BATCH, KVH, HD), (1, 2, 0, 3))
    all_keys = jnp.concatenate([kv_cache[0], draft_keys], axis=2).astype(jnp.float32)
    all_values = jnp.concatenate([kv_cache[1], draft_values], axis=2).astype(jnp.float32)
    scores = jnp.einsum('tbgjd,bgpd->tbgjp', queries, all_keys) * scale
    position = jnp.arange(CACHE + STEPS, dtype=jnp.int32)
    in_cache = position < CACHE
    cache_ok = position[None, :] < lengths[:, None]
    draft_ok = (position - CACHE)[None, :] <= jnp.arange(STEPS, dtype=jnp.int32)[:, None]
    visible = jnp.where(in_cache[None, None, :], cache_ok[None, :, :], draft_ok[:, None, :])
    visible = visible[:, :, None, None, :]
    highest = lax.optimization_barrier(jnp.max(jnp.where(visible, scores, -jnp.inf), axis=-1, keepdims=True))
    weights = jnp.where(visible, jnp.exp(scores - highest), 0.0)
    denominator = lax.optimization_barrier(jnp.sum(weights, axis=-1))
    numerator = jnp.einsum('tbgjp,bgpd->tbgjd', weights, all_values)
    attended = (numerator / denominator[..., None]).astype(jnp.bfloat16)
    attended = attended.reshape(STEPS * BATCH, H * HD)
    projected = jnp.dot(attended, out_weight, preferred_element_type=jnp.float32)
    carried = (residual.reshape(STEPS * BATCH, D).astype(jnp.float32) + projected).astype(jnp.bfloat16)
    wide = carried.astype(jnp.float32)
    mean_square = lax.optimization_barrier(jnp.mean(wide * wide, axis=1, keepdims=True))
    normed = (wide * lax.rsqrt(mean_square + 1e-05) * norm_gain.astype(jnp.float32)).astype(jnp.bfloat16)
    gate = jnp.dot(normed, gate_weight.T, preferred_element_type=jnp.float32)
    up_part = jnp.dot(normed, up_weight.T, preferred_element_type=jnp.float32)
    hidden = (jax.nn.silu(gate) * up_part).astype(jnp.bfloat16)
    down = jnp.dot(hidden, down_weight, preferred_element_type=jnp.float32)
    return (wide + down).astype(jnp.bfloat16).reshape(STEPS, BATCH, D)
```

```python
import functools
import math

import jax
import jax.numpy as jnp
from jax import lax
from jax.experimental import pallas as pl
from jax.experimental.pallas import tpu as pltpu
from jax.sharding import PartitionSpec as P

EPSILON = 1e-05
HIDE = -1e30
LANES = 128
MESH = pl.DeviceIdType.MESH
ROWS_BY_ROWS = (((1,), (1,)), ((), ()))
BF16 = jnp.bfloat16
F32 = jnp.float32


def dot(left, right):
    return jnp.dot(left, right, preferred_element_type=F32)


def dot_rows(left, right):
    return lax.dot_general(left, right, ROWS_BY_ROWS, preferred_element_type=F32)


def drain(ref, sem):
    pltpu.make_async_copy(ref, ref, sem).wait()


def layer_kernel(
    dims,
    query,
    draft,
    lengths,
    residual,
    gain,
    cache_hbm,
    out_hbm,
    gate_hbm,
    up_hbm,
    down_hbm,
    result,
    cache,
    out_w,
    gate_w,
    up_w,
    down_w,
    numer,
    stats,
    att_msg,
    att_in,
    heads,
    proj_msg,
    proj_in,
    gains,
    feats,
    half_wide,
    half_msg,
    half_in,
    pair_msg,
    down_in,
    cache_sem,
    weight_sem,
    send_sem,
    recv_sem,
    feat_sem,
    relay_sem,
    half_sem,
):
    ctx_n, kvh_n, planes, steps, batch = dims
    x_n = kvh_n // 2
    z_n = ctx_n // planes
    per_plane = z_n * x_n
    chips = ctx_n * x_n
    tokens = steps * batch
    shard_len = cache.shape[2]
    scale = 1.0 / math.sqrt(LANES)
    ctx = lax.axis_index("ctx")
    kvh = lax.axis_index("kvh")
    core = lax.rem(kvh, 2)
    chip = ctx * x_n + lax.div(kvh, 2)
    plane = lax.div(ctx, z_n)
    spot = lax.rem(chip, per_plane)
    partner = (ctx, kvh + 1 - 2 * core)

    def chip_device(at):
        return (lax.div(at, x_n), lax.rem(at, x_n) * 2 + core)

    def send(src, dst, at_send, at_recv, device):
        pltpu.make_async_remote_copy(
            src_ref=src,
            dst_ref=dst,
            send_sem=at_send,
            recv_sem=at_recv,
            device_id=device,
            device_id_type=MESH,
        ).start()

    cache_copies = []
    for b in range(batch):
        copy = pltpu.make_async_copy(cache_hbm.at[:, b], cache.at[:, b], cache_sem.at[b])
        copy.start()
        cache_copies.append(copy)
    weight_copies = []
    for at, (src, dst) in enumerate(
        ((out_hbm, out_w), (gate_hbm, gate_w), (up_hbm, up_w), (down_hbm, down_w))
    ):
        copy = pltpu.make_async_copy(src, dst, weight_sem.at[at])
        copy.start()
        weight_copies.append(copy)

    barrier = pltpu.get_barrier_semaphore()

    @pl.loop(1, chips)
    def _(i):
        pl.semaphore_signal(
            barrier, inc=1, device_id=chip_device(lax.rem(chip + i, chips)), device_id_type=MESH
        )

    @pl.loop(0, x_n)
    def _(i):
        pl.semaphore_signal(
            barrier, inc=1, device_id=(ctx, 2 * i + 1 - core), device_id_type=MESH
        )

    lane = lax.broadcasted_iota(jnp.int32, (ctx_n * steps, LANES), 1)
    position = ctx * shard_len + lax.broadcasted_iota(jnp.int32, (ctx_n * steps, shard_len), 1)
    draft_row = lax.broadcasted_iota(jnp.int32, (ctx_n * steps, tokens), 0)
    draft_col = lax.broadcasted_iota(jnp.int32, (ctx_n * steps, tokens), 1)
    draft_step = lax.div(draft_col, batch) + ctx * steps
    for b in range(batch):
        cache_copies[b].wait()
        q = query[b]
        seen = position < lengths[b]
        scores = jnp.where(seen, dot_rows(q, cache[0, b]) * scale, HIDE)
        draft_seen = (draft_step <= lax.rem(draft_row, steps)) & (
            lax.rem(draft_col, batch) == b
        )
        draft_scores = jnp.where(draft_seen, dot_rows(q, draft[0]) * scale, HIDE)
        top = jnp.maximum(
            jnp.max(scores, axis=1, keepdims=True), jnp.max(draft_scores, axis=1, keepdims=True)
        )
        top = top.astype(BF16).astype(F32)
        weights = jnp.where(seen, jnp.exp(scores - top), 0.0)
        draft_weights = jnp.where(draft_seen, jnp.exp(draft_scores - top), 0.0)
        total = jnp.sum(weights, axis=1, keepdims=True) + jnp.sum(
            draft_weights, axis=1, keepdims=True
        )
        values = dot(weights.astype(BF16), cache[1, b]) + dot(draft_weights.astype(BF16), draft[1])
        both = jnp.where(lane < 64, top, total)
        for h in range(ctx_n):
            rows = slice(h * steps, (h + 1) * steps)
            numer[h, b * steps : (b + 1) * steps, :] = values[rows]
            stats[h, b * steps : (b + 1) * steps, :] = both[rows]
    att_msg[:, 0:tokens, :] = numer[...].astype(BF16)
    wide = stats[...]
    high = wide.astype(BF16).astype(F32)
    lanes3 = lax.broadcasted_iota(jnp.int32, wide.shape, 2)
    att_msg[:, tokens : 2 * tokens, :] = jnp.where(lanes3 < 96, high, wide - high).astype(BF16)

    pl.semaphore_wait(barrier, chips - 1 + x_n)

    @pl.loop(1, ctx_n)
    def _(i):
        to = lax.rem(ctx + i, ctx_n)
        send(att_msg.at[to], att_in.at[ctx], send_sem.at[0], recv_sem.at[0], (to, kvh))

    att_in[ctx] = att_msg[ctx]
    gains[kvh, ctx] = gain[...]

    @pl.loop(1, ctx_n)
    def _(i):
        to = lax.rem(ctx + i, ctx_n)
        send(gains.at[kvh, ctx], gains.at[kvh, ctx], send_sem.at[1], recv_sem.at[1], (to, kvh))

    drain(att_in.at[0 : ctx_n - 1], recv_sem.at[0])
    parts = [att_in[i, tokens : 2 * tokens, :].astype(F32) for i in range(ctx_n)]
    tops = [jnp.broadcast_to(p[:, 0:1], (tokens, LANES)) for p in parts]
    highest = functools.reduce(jnp.maximum, tops)
    factors = [jnp.exp(t - highest) for t in tops]
    denominator = sum(f * (p[:, 64:65] + p[:, 96:97]) for f, p in zip(factors, parts))
    numerator = sum(
        f * att_in[i, 0:tokens, :].astype(F32) for i, f in enumerate(factors)
    )
    heads[ctx] = (numerator / denominator).astype(BF16)

    @pl.loop(1, ctx_n)
    def _(i):
        to = lax.rem(ctx + i, ctx_n)
        send(heads.at[ctx], heads.at[ctx], send_sem.at[2], recv_sem.at[2], (to, kvh))

    drain(gains.at[0, 0 : ctx_n - 1], recv_sem.at[1])

    @pl.loop(1, kvh_n)
    def _(i):
        to = lax.rem(kvh + i, kvh_n)
        send(gains.at[kvh], gains.at[kvh], send_sem.at[3], recv_sem.at[3], (ctx, to))

    weight_copies[0].wait()
    drain(heads.at[0 : ctx_n - 1], recv_sem.at[2])
    attended = jnp.concatenate([heads[i] for i in range(ctx_n)], axis=1)
    projected = dot(attended, out_w[...])
    for k in range(kvh_n):
        proj_msg[k] = projected[:, k * LANES : (k + 1) * LANES]

    @pl.loop(1, kvh_n)
    def _(i):
        to = lax.rem(kvh + i, kvh_n)
        send(proj_msg.at[to], proj_in.at[kvh], send_sem.at[4], recv_sem.at[4], (ctx, to))

    proj_in[kvh] = proj_msg[kvh]
    drain(proj_in.at[0 : kvh_n - 1], recv_sem.at[4])
    carried = residual[...].astype(F32)
    for k in range(kvh_n):
        carried = carried + proj_in[k]
    carried = carried.astype(BF16)
    feats[core, chip] = carried

    for d in range(planes):
        first = lax.rem(plane + d, planes) * per_plane

        @pl.loop(1 if d == 0 else 0, per_plane)
        def _(i):
            to = first + lax.rem(spot + i, per_plane)
            send(
                feats.at[core, chip],
                feats.at[core, chip],
                send_sem.at[5],
                feat_sem.at[plane],
                chip_device(to),
            )

    drain(gains.at[0 : kvh_n - 1], recv_sem.at[3])
    weight_copies[1].wait()
    weight_copies[2].wait()
    order = [0] + [d for d in (1, planes - 1, *range(2, planes - 1)) if d < planes]
    order = list(dict.fromkeys(order))
    width = per_plane * 2 * LANES
    gate = jnp.zeros((tokens, gate_w.shape[0]), F32)
    up = jnp.zeros((tokens, gate_w.shape[0]), F32)
    squares = jnp.zeros((tokens, LANES), F32)

    def relay(d):
        at = lax.rem(plane + d, planes)
        first = at * per_plane
        count = per_plane - 1 if d == 0 else per_plane
        drain(feats.at[core, pl.ds(first, count)], feat_sem.at[at])
        block = feats.at[core, pl.ds(first, per_plane)]
        send(block, block, send_sem.at[6], relay_sem.at[at], partner)

    relay(order[0])
    for n, d in enumerate(order):
        if n + 1 < planes:
            relay(order[n + 1])
        at = lax.rem(plane + d, planes)
        first = at * per_plane
        drain(feats.at[1 - core, pl.ds(first, per_plane)], relay_sem.at[at])
        pieces = []
        for s in range(per_plane):
            for c in range(2):
                piece = feats[c, first + s].astype(F32)
                squares = squares + piece * piece
                scaled = piece * gains[s % x_n * 2 + c, at * z_n + s // x_n]
                pieces.append(scaled.astype(BF16))
        rows = jnp.concatenate(pieces, axis=1)
        columns = pl.ds(pl.multiple_of(at * width, width), width)
        gate = gate + dot_rows(rows, gate_w[:, columns])
        up = up + dot_rows(rows, up_w[:, columns])
    mean_square = jnp.sum(squares, axis=1, keepdims=True) / (chips * 2 * LANES)
    inverse = lax.rsqrt(mean_square + EPSILON)
    gate = gate * inverse
    up = up * inverse
    hidden = (gate / (1.0 + jnp.exp(-gate)) * up).astype(BF16)

    weight_copies[3].wait()
    order = order[::-1]

    def halves(n):
        at = lax.rem(plane + order[n], planes)
        columns = pl.ds(pl.multiple_of(at * width, width), width)
        block = dot(hidden, down_w[:, columns])
        for s in range(per_plane):
            for c in range(2):
                piece = block[:, (2 * s + c) * LANES : (2 * s + c + 1) * LANES]
                half_wide[n, c, s] = piece
                half_msg[n, c, s] = piece.astype(BF16)
        send(half_msg.at[n, 1 - core], half_in.at[n], send_sem.at[7], half_sem.at[n], partner)

    def spread(n):
        d = order[n]
        first = lax.rem(plane + d, planes) * per_plane
        drain(half_in.at[n], half_sem.at[n])
        pair_msg[n] = (half_wide[n, core] + half_in[n].astype(F32)).astype(BF16)

        @pl.loop(1 if d == 0 else 0, per_plane)
        def _(i):
            to = lax.rem(spot + i, per_plane)
            send(
                pair_msg.at[n, to],
                down_in.at[chip],
                send_sem.at[8],
                recv_sem.at[5],
                chip_device(first + to),
            )

    for n in range(planes):
        halves(n)
        if n >= 1:
            spread(n - 1)
    spread(planes - 1)
    down_in[chip] = pair_msg[planes - 1, spot]
    drain(down_in.at[0 : chips - 1], recv_sem.at[5])
    final = carried.astype(F32) + jnp.sum(down_in[...].astype(F32), axis=0)
    result[...] = final.astype(BF16)

    drain(att_in.at[0 : ctx_n - 1], send_sem.at[0])
    drain(gains.at[0, 0 : ctx_n - 1], send_sem.at[1])
    drain(heads.at[0 : ctx_n - 1], send_sem.at[2])
    drain(gains.at[0 : kvh_n - 1], send_sem.at[3])
    drain(proj_in.at[0 : kvh_n - 1], send_sem.at[4])
    drain(down_in.at[0 : chips - 1], send_sem.at[5])
    drain(feats.at[0], send_sem.at[6])
    drain(feats.at[0], send_sem.at[7])
    drain(down_in.at[0 : chips - 1], send_sem.at[8])


def per_device(ctx_n, kvh_n, planes, *arguments):
    (
        query,
        new_kv,
        kv_cache,
        lengths,
        residual,
        out_weight,
        norm_gain,
        gate_weight,
        up_weight,
        down_weight,
    ) = arguments
    steps, batch, query_width = query.shape
    heads = query_width // LANES
    assert heads == ctx_n and kv_cache.shape[2] == 1
    tokens = steps * batch
    chips = ctx_n * kvh_n // 2
    per_plane = chips // planes
    queries = query.reshape(steps, batch, heads, LANES).transpose(1, 2, 0, 3)
    queries = queries.reshape(batch, heads * steps, LANES)
    cache = kv_cache.reshape(2, batch, kv_cache.shape[3], LANES)
    vmem = pl.BlockSpec(memory_space=pltpu.VMEM)
    smem = pl.BlockSpec(memory_space=pltpu.SMEM)
    far = pl.BlockSpec(memory_space=pl.ANY)
    dma = pltpu.SemaphoreType.DMA
    out = pl.pallas_call(
        functools.partial(layer_kernel, (ctx_n, kvh_n, planes, steps, batch)),
        out_shape=jax.ShapeDtypeStruct((tokens, LANES), BF16),
        in_specs=[vmem, vmem, smem, vmem, vmem, far, far, far, far, far],
        out_specs=vmem,
        scratch_shapes=[
            pltpu.VMEM(cache.shape, BF16),
            pltpu.VMEM(out_weight.shape, BF16),
            pltpu.VMEM(gate_weight.shape, BF16),
            pltpu.VMEM(up_weight.shape, BF16),
            pltpu.VMEM(down_weight.shape, BF16),
            pltpu.VMEM((ctx_n, tokens, LANES), F32),
            pltpu.VMEM((ctx_n, tokens, LANES), F32),
            pltpu.VMEM((ctx_n, 2 * tokens, LANES), BF16),
            pltpu.VMEM((ctx_n, 2 * tokens, LANES), BF16),
            pltpu.VMEM((ctx_n, tokens, LANES), BF16),
            pltpu.VMEM((kvh_n, tokens, LANES), F32),
            pltpu.VMEM((kvh_n, tokens, LANES), F32),
            pltpu.VMEM((kvh_n, ctx_n, 1, LANES), F32),
            pltpu.VMEM((2, chips, tokens, LANES), BF16),
            pltpu.VMEM((planes, 2, per_plane, tokens, LANES), F32),
            pltpu.VMEM((planes, 2, per_plane, tokens, LANES), BF16),
            pltpu.VMEM((planes, per_plane, tokens, LANES), BF16),
            pltpu.VMEM((planes, per_plane, tokens, LANES), BF16),
            pltpu.VMEM((chips, tokens, LANES), BF16),
            dma((batch,)),
            dma((4,)),
            dma((9,)),
            dma((6,)),
            dma((planes,)),
            dma((planes,)),
            dma((planes,)),
        ],
        compiler_params=pltpu.CompilerParams(
            collective_id=0, has_side_effects=True, vmem_limit_bytes=56 * 2**20
        ),
        name="layer",
    )(
        queries,
        new_kv.reshape(2, tokens, LANES),
        lengths,
        residual.transpose(1, 0, 2).reshape(tokens, LANES),
        norm_gain.reshape(1, LANES),
        cache,
        out_weight,
        gate_weight,
        up_weight,
        down_weight,
    )
    return out.reshape(batch, steps, LANES).transpose(1, 0, 2)


def solution(mesh):
    ctx_n, kvh_n = mesh.shape["ctx"], mesh.shape["kvh"]
    planes = 4 if ctx_n % 4 == 0 and ctx_n > 4 else 2
    return jax.shard_map(
        functools.partial(per_device, ctx_n, kvh_n, planes),
        mesh=mesh,
        in_specs=(
            P(None, None, "kvh"),
            P(None, None, None, "kvh"),
            P(None, None, "kvh", "ctx", None),
            P(),
            P(None, None, ("ctx", "kvh")),
            P("kvh", "ctx"),
            P(("ctx", "kvh")),
            P(("ctx", "kvh"), None),
            P(("ctx", "kvh"), None),
            P(("ctx", "kvh"), None),
        ),
        out_specs=P(None, None, ("ctx", "kvh")),
        check_vma=False,
    )
```

```python
import functools
import math

import jax
import jax.numpy as jnp
from jax import lax
from jax.experimental import pallas as pl
from jax.experimental.pallas import tpu as pltpu
from jax.sharding import PartitionSpec as P

EPSILON = 1e-05
HIDE = -1e30
LANES = 128
MESH = pl.DeviceIdType.MESH
ROWS_BY_ROWS = (((1,), (1,)), ((), ()))
BF16 = jnp.bfloat16
F32 = jnp.float32


def dot(left, right):
    return jnp.dot(left, right, preferred_element_type=F32)


def dot_rows(left, right):
    return lax.dot_general(left, right, ROWS_BY_ROWS, preferred_element_type=F32)


def drain(ref, sem):
    pltpu.make_async_copy(ref, ref, sem).wait()


def layer_kernel(
    dims,
    query,
    draft,
    lengths,
    residual,
    gain,
    cache_hbm,
    out_hbm,
    gate_hbm,
    up_hbm,
    down_hbm,
    result,
    cache,
    out_w,
    gate_up_w,
    down_w,
    queries,
    numer,
    stats,
    att_msg,
    att_in,
    heads,
    proj_msg,
    proj_in,
    gains,
    feats,
    half_wide,
    half_msg,
    half_in,
    pair_msg,
    down_in,
    cache_sem,
    weight_sem,
    send_sem,
    recv_sem,
    head_sem,
    feat_sem,
    relay_sem,
    half_sem,
):
    ctx_n, kvh_n, planes, steps, batch = dims
    x_n = kvh_n // 2
    z_n = ctx_n // planes
    chips = ctx_n * x_n
    tokens = steps * batch
    shard_len = cache.shape[2]
    units = down_w.shape[0]
    scale = 1.0 / math.sqrt(LANES)
    ctx = lax.axis_index("ctx")
    kvh = lax.axis_index("kvh")
    core = lax.rem(kvh, 2)
    x = lax.div(kvh, 2)
    chip = ctx * x_n + x
    plane = lax.div(ctx, z_n)
    place = lax.rem(ctx, z_n)
    partner = (ctx, kvh + 1 - 2 * core)

    def far(dy, dz):
        return min(dy, planes - dy) + min(dz, z_n - dz)

    offsets = sorted(
        ((dy, dz) for dy in range(planes) for dz in range(z_n)), key=lambda o: (far(*o), o)
    )
    opposite = [offsets.index((-dy % planes, -dz % z_n)) for dy, dz in offsets]
    hops = [far(*o) for o in offsets]
    class_n = hops[-1] + 1
    bounds = [(hops.index(k), hops.index(k) + hops.count(k)) for k in range(class_n)]
    ctx_at = [
        lax.rem(plane + dy, planes) * z_n + lax.rem(place + dz, z_n) for dy, dz in offsets
    ]

    def send(src, dst, at_send, at_recv, device):
        pltpu.make_async_remote_copy(
            src_ref=src,
            dst_ref=dst,
            send_sem=at_send,
            recv_sem=at_recv,
            device_id=device,
            device_id_type=MESH,
        ).start()

    cache_copies = []
    for b in range(batch):
        copy = pltpu.make_async_copy(cache_hbm.at[:, b], cache.at[:, b], cache_sem.at[b])
        copy.start()
        cache_copies.append(copy)

    barrier = pltpu.get_barrier_semaphore()

    @pl.loop(1, chips)
    def _(i):
        at = lax.rem(chip + i, chips)
        pl.semaphore_signal(
            barrier,
            inc=1,
            device_id=(lax.div(at, x_n), lax.rem(at, x_n) * 2 + core),
            device_id_type=MESH,
        )

    @pl.loop(0, x_n)
    def _(i):
        pl.semaphore_signal(
            barrier, inc=1, device_id=(ctx, 2 * i + 1 - core), device_id_type=MESH
        )

    for t in range(steps):
        row = query[t].astype(F32)
        for h in range(ctx_n):
            at = h * tokens + t * batch
            queries[at : at + batch, :] = row[:, h * LANES : (h + 1) * LANES]

    lane = lax.broadcasted_iota(jnp.int32, (ctx_n * steps, LANES), 1)
    position = ctx * shard_len + lax.broadcasted_iota(jnp.int32, (ctx_n * steps, shard_len), 1)
    draft_row = lax.broadcasted_iota(jnp.int32, (ctx_n * steps, tokens), 0)
    draft_col = lax.broadcasted_iota(jnp.int32, (ctx_n * steps, tokens), 1)
    draft_step = lax.div(draft_col, batch) + ctx * steps
    weight_copies = []
    for b in range(batch):
        cache_copies[b].wait()
        if b == batch - 1:
            for at, (src, dst) in enumerate(
                (
                    (out_hbm, out_w),
                    (gate_hbm, gate_up_w.at[0:units]),
                    (up_hbm, gate_up_w.at[units : 2 * units]),
                    (down_hbm, down_w),
                )
            ):
                copy = pltpu.make_async_copy(src, dst, weight_sem.at[at])
                copy.start()
                weight_copies.append(copy)
        mine = pl.ds(b, ctx_n * steps, stride=batch)
        q = queries[mine, :].astype(BF16)
        seen = position < lengths[b]
        scores = jnp.where(seen, dot_rows(q, cache[0, b]) * scale, HIDE)
        draft_seen = (draft_step <= lax.rem(draft_row, steps)) & (
            lax.rem(draft_col, batch) == b
        )
        draft_scores = jnp.where(draft_seen, dot_rows(q, draft[0]) * scale, HIDE)
        top = jnp.maximum(
            jnp.max(scores, axis=1, keepdims=True), jnp.max(draft_scores, axis=1, keepdims=True)
        )
        top = top.astype(BF16).astype(F32)
        weights = jnp.where(seen, jnp.exp(scores - top), 0.0)
        draft_weights = jnp.where(draft_seen, jnp.exp(draft_scores - top), 0.0)
        total = jnp.sum(weights, axis=1, keepdims=True) + jnp.sum(
            draft_weights, axis=1, keepdims=True
        )
        numer[mine, :] = dot(weights.astype(BF16), cache[1, b]) + dot(
            draft_weights.astype(BF16), draft[1]
        )
        stats[mine, :] = jnp.where(lane < 64, top, total)
    by_head = (ctx_n, tokens, LANES)
    att_msg[:, 0:tokens, :] = numer[...].reshape(by_head).astype(BF16)
    wide = stats[...].reshape(by_head)
    high = wide.astype(BF16).astype(F32)
    lanes3 = lax.broadcasted_iota(jnp.int32, by_head, 2)
    att_msg[:, tokens : 2 * tokens, :] = jnp.where(lanes3 < 96, high, wide - high).astype(BF16)

    pl.semaphore_wait(barrier, chips - 1 + x_n)

    for n in range(1, ctx_n):
        to = ctx_at[n]
        send(att_msg.at[to], att_in.at[opposite[n]], send_sem.at[0], recv_sem.at[0], (to, kvh))
    att_in[0] = att_msg[ctx]
    gains[kvh, ctx] = gain[...]

    @pl.loop(1, ctx_n)
    def _(i):
        to = lax.rem(ctx + i, ctx_n)
        send(gains.at[kvh, ctx], gains.at[kvh, ctx], send_sem.at[1], recv_sem.at[1], (to, kvh))

    drain(att_in.at[0 : ctx_n - 1], recv_sem.at[0])
    parts = [att_in[i, tokens : 2 * tokens, :].astype(F32) for i in range(ctx_n)]
    tops = [jnp.broadcast_to(p[:, 0:1], (tokens, LANES)) for p in parts]
    highest = functools.reduce(jnp.maximum, tops)
    factors = [jnp.exp(t - highest) for t in tops]
    denominator = sum(f * (p[:, 64:65] + p[:, 96:97]) for f, p in zip(factors, parts))
    numerator = sum(
        f * att_in[i, 0:tokens, :].astype(F32) for i, f in enumerate(factors)
    )
    heads[0] = (numerator / denominator).astype(BF16)

    for n in range(1, ctx_n):
        send(
            heads.at[0],
            heads.at[opposite[n]],
            send_sem.at[2],
            head_sem.at[hops[n]],
            (ctx_at[n], kvh),
        )

    drain(gains.at[0, 0 : ctx_n - 1], recv_sem.at[1])

    @pl.loop(1, kvh_n)
    def _(i):
        to = lax.rem(kvh + i, kvh_n)
        send(gains.at[kvh], gains.at[kvh], send_sem.at[3], recv_sem.at[3], (ctx, to))

    weight_copies[0].wait()
    projected = jnp.zeros((tokens, kvh_n * LANES), F32)
    for group in ([0, 1], [2], list(range(3, class_n))):
        group = [k for k in group if k < class_n]
        if not group:
            continue
        low, high = bounds[group[0]][0], bounds[group[-1]][1]
        for k in group:
            if k > 0:
                drain(heads.at[bounds[k][0] : bounds[k][1]], head_sem.at[k])
        attended = jnp.concatenate([heads[n] for n in range(low, high)], axis=1)
        rows = jnp.concatenate(
            [
                out_w[pl.ds(pl.multiple_of(ctx_at[n] * LANES, LANES), LANES), :]
                for n in range(low, high)
            ],
            axis=0,
        )
        projected = projected + dot(attended, rows)
    for k in range(kvh_n):
        proj_msg[k] = projected[:, k * LANES : (k + 1) * LANES]

    @pl.loop(1, kvh_n)
    def _(i):
        to = lax.rem(kvh + i, kvh_n)
        send(proj_msg.at[to], proj_in.at[kvh], send_sem.at[4], recv_sem.at[4], (ctx, to))

    proj_in[kvh] = proj_msg[kvh]
    drain(gains.at[0 : kvh_n - 1], recv_sem.at[3])
    drain(proj_in.at[0 : kvh_n - 1], recv_sem.at[4])
    carried = residual[...].astype(F32)
    for k in range(kvh_n):
        carried = carried + proj_in[k]
    carried = carried.astype(BF16)
    feats[core, 0, x] = carried

    for n in range(ctx_n):

        @pl.loop(1 if n == 0 else 0, x_n)
        def _(i):
            send(
                feats.at[core, 0, x],
                feats.at[core, opposite[n], x],
                send_sem.at[5],
                feat_sem.at[hops[n]],
                (ctx_at[n], lax.rem(x + i, x_n) * 2 + core),
            )

    width = kvh_n * LANES
    products = jnp.zeros((tokens, 2 * units), F32)
    squares = jnp.zeros((tokens, LANES), F32)

    def relay(k):
        low, high = bounds[k]
        drain(feats.at[core, 0, 0 : x_n - 1] if k == 0 else feats.at[core, low:high], feat_sem.at[k])
        block = feats.at[core, low:high]
        send(block, block, send_sem.at[6], relay_sem.at[k], partner)

    weight_copies[1].wait()
    weight_copies[2].wait()
    relay(0)
    for k in range(class_n):
        if k + 1 < class_n:
            relay(k + 1)
        low, high = bounds[k]
        drain(feats.at[1 - core, low:high], relay_sem.at[k])
        for n in range(low, high):
            pieces = []
            for j in range(kvh_n):
                piece = feats[j % 2, n, j // 2].astype(F32)
                squares = squares + piece * piece
                pieces.append((piece * gains[j, ctx_at[n]]).astype(BF16))
            rows = jnp.concatenate(pieces, axis=1)
            columns = pl.ds(pl.multiple_of(ctx_at[n] * width, width), width)
            products = products + dot_rows(rows, gate_up_w[:, columns])
    mean_square = jnp.sum(squares, axis=1, keepdims=True) / (chips * 2 * LANES)
    products = products * lax.rsqrt(mean_square + EPSILON)
    gate = products[:, 0:units]
    up = products[:, units : 2 * units]
    hidden = (gate / (1.0 + jnp.exp(-gate)) * up).astype(BF16)

    weight_copies[3].wait()
    groups = [bounds[k] for k in range(class_n - 1, 1, -1)] + [(0, bounds[1][1])]

    def halves(g):
        low, high = groups[g]
        for n in range(low, high):
            columns = pl.ds(pl.multiple_of(ctx_at[n] * width, width), width)
            block = dot(hidden, down_w[:, columns])
            for j in range(kvh_n):
                piece = block[:, j * LANES : (j + 1) * LANES]
                half_wide[j % 2, n, j // 2] = piece
                half_msg[j % 2, n, j // 2] = piece.astype(BF16)
        send(
            half_msg.at[1 - core, low:high],
            half_in.at[low:high],
            send_sem.at[7],
            half_sem.at[g],
            partner,
        )

    def spread(g):
        low, high = groups[g]
        drain(half_in.at[low:high], half_sem.at[g])
        pair_msg[low:high] = (half_wide[core, low:high] + half_in[low:high].astype(F32)).astype(
            BF16
        )
        for n in range(low, high):

            @pl.loop(1 if n == 0 else 0, x_n)
            def _(i):
                to = lax.rem(x + i, x_n)
                send(
                    pair_msg.at[n, to],
                    down_in.at[chip],
                    send_sem.at[8],
                    recv_sem.at[5],
                    (ctx_at[n], to * 2 + core),
                )

    for g in range(len(groups)):
        halves(g)
        if g >= 1:
            spread(g - 1)
    spread(len(groups) - 1)
    down_in[chip] = pair_msg[0, x]
    drain(down_in.at[0 : chips - 1], recv_sem.at[5])
    final = carried.astype(F32) + jnp.sum(down_in[...].astype(F32), axis=0)
    result[...] = final.astype(BF16)

    drain(att_in.at[0 : ctx_n - 1], send_sem.at[0])
    drain(gains.at[0, 0 : ctx_n - 1], send_sem.at[1])
    drain(heads.at[0 : ctx_n - 1], send_sem.at[2])
    drain(gains.at[0 : kvh_n - 1], send_sem.at[3])
    drain(proj_in.at[0 : kvh_n - 1], send_sem.at[4])
    drain(down_in.at[0 : chips - 1], send_sem.at[5])
    drain(feats.at[0], send_sem.at[6])
    drain(half_in, send_sem.at[7])
    drain(down_in.at[0 : chips - 1], send_sem.at[8])


def per_device(ctx_n, kvh_n, planes, *arguments):
    (
        query,
        new_kv,
        kv_cache,
        lengths,
        residual,
        out_weight,
        norm_gain,
        gate_weight,
        up_weight,
        down_weight,
    ) = arguments
    steps, batch, query_width = query.shape
    heads = query_width // LANES
    assert heads == ctx_n and kv_cache.shape[2] == 1
    tokens = steps * batch
    chips = ctx_n * kvh_n // 2
    x_n = kvh_n // 2
    classes = planes // 2 + ctx_n // planes // 2 + 1
    cache = kv_cache.reshape(2, batch, kv_cache.shape[3], LANES)
    units = gate_weight.shape[0]
    vmem = pl.BlockSpec(memory_space=pltpu.VMEM)
    smem = pl.BlockSpec(memory_space=pltpu.SMEM)
    far = pl.BlockSpec(memory_space=pl.ANY)
    dma = pltpu.SemaphoreType.DMA
    out = pl.pallas_call(
        functools.partial(layer_kernel, (ctx_n, kvh_n, planes, steps, batch)),
        out_shape=jax.ShapeDtypeStruct((tokens, LANES), BF16),
        in_specs=[vmem, vmem, smem, vmem, vmem, far, far, far, far, far],
        out_specs=vmem,
        scratch_shapes=[
            pltpu.VMEM(cache.shape, BF16),
            pltpu.VMEM(out_weight.shape, BF16),
            pltpu.VMEM((2 * units, gate_weight.shape[1]), BF16),
            pltpu.VMEM(down_weight.shape, BF16),
            pltpu.VMEM((ctx_n * tokens, LANES), F32),
            pltpu.VMEM((ctx_n * tokens, LANES), F32),
            pltpu.VMEM((ctx_n * tokens, LANES), F32),
            pltpu.VMEM((ctx_n, 2 * tokens, LANES), BF16),
            pltpu.VMEM((ctx_n, 2 * tokens, LANES), BF16),
            pltpu.VMEM((ctx_n, tokens, LANES), BF16),
            pltpu.VMEM((kvh_n, tokens, LANES), F32),
            pltpu.VMEM((kvh_n, tokens, LANES), F32),
            pltpu.VMEM((kvh_n, ctx_n, 1, LANES), F32),
            pltpu.VMEM((2, ctx_n, x_n, tokens, LANES), BF16),
            pltpu.VMEM((2, ctx_n, x_n, tokens, LANES), F32),
            pltpu.VMEM((2, ctx_n, x_n, tokens, LANES), BF16),
            pltpu.VMEM((ctx_n, x_n, tokens, LANES), BF16),
            pltpu.VMEM((ctx_n, x_n, tokens, LANES), BF16),
            pltpu.VMEM((chips, tokens, LANES), BF16),
            dma((batch,)),
            dma((4,)),
            dma((9,)),
            dma((6,)),
            dma((classes,)),
            dma((classes,)),
            dma((classes,)),
            dma((classes,)),
        ],
        compiler_params=pltpu.CompilerParams(
            collective_id=0, has_side_effects=True, vmem_limit_bytes=56 * 2**20
        ),
        name="layer",
    )(
        query,
        new_kv.reshape(2, tokens, LANES),
        lengths,
        residual.reshape(tokens, LANES),
        norm_gain.reshape(1, LANES),
        cache,
        out_weight,
        gate_weight,
        up_weight,
        down_weight,
    )
    return out.reshape(steps, batch, LANES)


def solution(mesh):
    ctx_n, kvh_n = mesh.shape["ctx"], mesh.shape["kvh"]
    planes = 4 if ctx_n % 4 == 0 and ctx_n > 4 else 2
    return jax.shard_map(
        functools.partial(per_device, ctx_n, kvh_n, planes),
        mesh=mesh,
        in_specs=(
            P(None, None, "kvh"),
            P(None, None, None, "kvh"),
            P(None, None, "kvh", "ctx", None),
            P(),
            P(None, None, ("ctx", "kvh")),
            P("kvh", "ctx"),
            P(("ctx", "kvh")),
            P(("ctx", "kvh"), None),
            P(("ctx", "kvh"), None),
            P(("ctx", "kvh"), None),
        ),
        out_specs=P(None, None, ("ctx", "kvh")),
        check_vma=False,
    )
```

```python
import functools
import itertools
import math

import jax
import jax.numpy as jnp
from jax import lax
from jax.experimental import pallas as pl
from jax.experimental.pallas import tpu as pltpu
from jax.sharding import PartitionSpec as P

EPSILON = 1e-05
HIDE = -1e30
LANES = 128
MESH = pl.DeviceIdType.MESH
ROWS_BY_ROWS = (((1,), (1,)), ((), ()))
BF16 = jnp.bfloat16
F32 = jnp.float32


def dot(left, right):
    return jnp.dot(left, right, preferred_element_type=F32)


def dot_rows(left, right):
    return lax.dot_general(left, right, ROWS_BY_ROWS, preferred_element_type=F32)


def drain(ref, sem):
    pltpu.make_async_copy(ref, ref, sem).wait()


def chip_groups(*sizes):
    longest = sum(size // 2 for size in sizes)
    return [(0, 1), *((k, k) for k in range(2, longest - 1)), (longest - 1, longest)]


def layer_kernel(
    dims,
    query_hbm,
    draft_hbm,
    lengths_hbm,
    residual_hbm,
    gain_hbm,
    cache_hbm,
    out_hbm,
    gate_hbm,
    up_hbm,
    down_hbm,
    result,
    query,
    draft,
    lengths,
    residual,
    gain,
    cache,
    out_w,
    gate_up_w,
    down_w,
    queries,
    numer,
    stats,
    att_msg,
    att_in,
    heads,
    proj_msg,
    proj_in,
    gains,
    feats,
    half_wide,
    half_msg,
    half_in,
    pair_msg,
    down_in,
    input_sem,
    cache_sem,
    weight_sem,
    send_sem,
    recv_sem,
    part_sem,
    head_sem,
    feat_sem,
    relay_sem,
    half_sem,
):
    ctx_n, kvh_n, planes, steps, batch = dims
    x_n = kvh_n // 2
    z_n = ctx_n // planes
    chips = ctx_n * x_n
    tokens = steps * batch
    shard_len = cache.shape[2]
    units = down_w.shape[0]
    scale = 1.0 / math.sqrt(LANES)
    ctx = lax.axis_index("ctx")
    kvh = lax.axis_index("kvh")
    core = lax.rem(kvh, 2)
    x = lax.div(kvh, 2)
    chip = ctx * x_n + x
    plane = lax.div(ctx, z_n)
    place = lax.rem(ctx, z_n)
    partner = (ctx, kvh + 1 - 2 * core)

    def ring(at, size):
        return min(at, size - at)

    def ordered(*sizes):
        at = itertools.product(*(range(size) for size in sizes))
        hops = lambda o: sum(ring(a, size) for a, size in zip(o, sizes))
        offsets = sorted(at, key=lambda o: (hops(o), o))
        opposite = [
            offsets.index(tuple(-a % size for a, size in zip(o, sizes))) for o in offsets
        ]
        return offsets, opposite, [hops(o) for o in offsets]

    def ctx_of(dy, dz):
        return lax.rem(plane + dy, planes) * z_n + lax.rem(place + dz, z_n)

    def span(hops, low, high):
        inside = [n for n, h in enumerate(hops) if low <= h <= high]
        return inside[0], inside[-1] + 1

    offsets, opposite, hops = ordered(planes, z_n)
    ctx_at = [ctx_of(*o) for o in offsets]
    chip_offsets, chip_opposite, chip_hops = ordered(planes, z_n, x_n)
    chip_at = [(ctx_of(dy, dz), lax.rem(x + dx, x_n)) for dy, dz, dx in chip_offsets]
    cuts = chip_groups(planes, z_n, x_n)
    groups = [span(chip_hops, low, high) for low, high in cuts]
    group_at = [[low <= h <= high for low, high in cuts].index(True) for h in chip_hops]

    def send(src, dst, at_send, at_recv, device):
        pltpu.make_async_remote_copy(
            src_ref=src,
            dst_ref=dst,
            send_sem=at_send,
            recv_sem=at_recv,
            device_id=device,
            device_id_type=MESH,
        ).start()

    inputs = []
    for at, (src, dst) in enumerate(
        (
            (query_hbm, query),
            (draft_hbm, draft),
            (lengths_hbm, lengths),
            (residual_hbm, residual),
            (gain_hbm, gain),
        )
    ):
        copy = pltpu.make_async_copy(src, dst, input_sem.at[at])
        copy.start()
        inputs.append(copy)
    cache_copies = []
    for b in range(batch):
        copy = pltpu.make_async_copy(cache_hbm.at[:, b], cache.at[:, b], cache_sem.at[b])
        copy.start()
        cache_copies.append(copy)

    barrier = pltpu.get_barrier_semaphore()

    @pl.loop(1, ctx_n)
    def _(i):
        pl.semaphore_signal(
            barrier, inc=1, device_id=(lax.rem(ctx + i, ctx_n), kvh), device_id_type=MESH
        )

    @pl.loop(1, kvh_n)
    def _(i):
        pl.semaphore_signal(
            barrier, inc=1, device_id=(ctx, lax.rem(kvh + i, kvh_n)), device_id_type=MESH
        )

    for copy in inputs:
        copy.wait()

    for t in range(steps):
        row = query[t].astype(F32)
        for h in range(ctx_n):
            at = h * tokens + t * batch
            queries[at : at + batch, :] = row[:, h * LANES : (h + 1) * LANES]

    lane = lax.broadcasted_iota(jnp.int32, (ctx_n * steps, LANES), 1)
    position = ctx * shard_len + lax.broadcasted_iota(jnp.int32, (ctx_n * steps, shard_len), 1)
    draft_row = lax.broadcasted_iota(jnp.int32, (ctx_n * steps, tokens), 0)
    draft_col = lax.broadcasted_iota(jnp.int32, (ctx_n * steps, tokens), 1)
    draft_step = lax.div(draft_col, batch) + ctx * steps
    weight_copies = []
    for b in range(batch):
        cache_copies[b].wait()
        if b == batch - 1:
            for at, (src, dst) in enumerate(
                (
                    (out_hbm, out_w),
                    (gate_hbm, gate_up_w.at[0:units]),
                    (up_hbm, gate_up_w.at[units : 2 * units]),
                    (down_hbm, down_w),
                )
            ):
                copy = pltpu.make_async_copy(src, dst, weight_sem.at[at])
                copy.start()
                weight_copies.append(copy)
        mine = pl.ds(b, ctx_n * steps, stride=batch)
        q = queries[mine, :].astype(BF16)
        seen = position < lengths[b]
        scores = jnp.where(seen, dot_rows(q, cache[0, b]) * scale, HIDE)
        draft_seen = (draft_step <= lax.rem(draft_row, steps)) & (
            lax.rem(draft_col, batch) == b
        )
        draft_scores = jnp.where(draft_seen, dot_rows(q, draft[0]) * scale, HIDE)
        top = jnp.maximum(
            jnp.max(scores, axis=1, keepdims=True), jnp.max(draft_scores, axis=1, keepdims=True)
        )
        top = top.astype(BF16).astype(F32)
        weights = jnp.where(seen, jnp.exp(scores - top), 0.0)
        draft_weights = jnp.where(draft_seen, jnp.exp(draft_scores - top), 0.0)
        total = jnp.sum(weights, axis=1, keepdims=True) + jnp.sum(
            draft_weights, axis=1, keepdims=True
        )
        numer[mine, :] = dot(weights.astype(BF16), cache[1, b]) + dot(
            draft_weights.astype(BF16), draft[1]
        )
        stats[mine, :] = jnp.where(lane < 64, top, total)
    by_head = (ctx_n, tokens, LANES)
    att_msg[:, 0:tokens, :] = numer[...].reshape(by_head).astype(BF16)
    wide = stats[...].reshape(by_head)
    high = wide.astype(BF16).astype(F32)
    lanes3 = lax.broadcasted_iota(jnp.int32, by_head, 2)
    att_msg[:, tokens : 2 * tokens, :] = jnp.where(lanes3 < 96, high, wide - high).astype(BF16)

    pl.semaphore_wait(barrier, ctx_n + kvh_n - 2)

    for n in range(1, ctx_n):
        to = ctx_at[n]
        send(
            att_msg.at[to],
            att_in.at[opposite[n]],
            send_sem.at[0],
            part_sem.at[0 if hops[n] <= 2 else 1],
            (to, kvh),
        )
    att_in[0] = att_msg[ctx]
    gains[kvh, ctx] = gain[...]

    @pl.loop(1, ctx_n)
    def _(i):
        to = lax.rem(ctx + i, ctx_n)
        send(gains.at[kvh, ctx], gains.at[kvh, ctx], send_sem.at[1], recv_sem.at[1], (to, kvh))

    def merged(low, high):
        parts = [att_in[i, tokens : 2 * tokens, :].astype(F32) for i in range(low, high)]
        tops = [jnp.broadcast_to(p[:, 0:1], (tokens, LANES)) for p in parts]
        highest = functools.reduce(jnp.maximum, tops)
        factors = [jnp.exp(t - highest) for t in tops]
        denominator = sum(f * (p[:, 64:65] + p[:, 96:97]) for f, p in zip(factors, parts))
        numerator = sum(
            f * att_in[low + i, 0:tokens, :].astype(F32) for i, f in enumerate(factors)
        )
        return highest, denominator, numerator

    low, high = span(hops, 0, 2)
    drain(att_in.at[0 : high - 1], part_sem.at[0])
    highest, denominator, numerator = merged(low, high)
    if high < ctx_n:
        drain(att_in.at[high:ctx_n], part_sem.at[1])
        highest2, denominator2, numerator2 = merged(high, ctx_n)
        top = jnp.maximum(highest, highest2)
        factor, factor2 = jnp.exp(highest - top), jnp.exp(highest2 - top)
        denominator = factor * denominator + factor2 * denominator2
        numerator = factor * numerator + factor2 * numerator2
    heads[0] = (numerator / denominator).astype(BF16)

    for n in range(1, ctx_n):
        send(
            heads.at[0],
            heads.at[opposite[n]],
            send_sem.at[2],
            head_sem.at[max(hops[n] - 1, 0)],
            (ctx_at[n], kvh),
        )

    drain(gains.at[0, 0 : ctx_n - 1], recv_sem.at[1])

    @pl.loop(1, kvh_n)
    def _(i):
        to = lax.rem(kvh + i, kvh_n)
        send(gains.at[kvh], gains.at[kvh], send_sem.at[3], recv_sem.at[3], (ctx, to))

    weight_copies[0].wait()
    projected = jnp.zeros((tokens, kvh_n * LANES), F32)
    for at, (first, last) in enumerate(((0, 1), (2, 2), (3, hops[-1]))):
        if first > last:
            continue
        low, high = span(hops, first, last)
        for k in range(max(first, 1), last + 1):
            start, end = span(hops, k, k)
            drain(heads.at[start:end], head_sem.at[k - 1])
        attended = jnp.concatenate([heads[n] for n in range(low, high)], axis=1)
        rows = jnp.concatenate(
            [
                out_w[pl.ds(pl.multiple_of(ctx_at[n] * LANES, LANES), LANES), :]
                for n in range(low, high)
            ],
            axis=0,
        )
        projected = projected + dot(attended, rows)
    for k in range(kvh_n):
        proj_msg[k] = projected[:, k * LANES : (k + 1) * LANES].astype(BF16)

    @pl.loop(1, kvh_n)
    def _(i):
        to = lax.rem(kvh + i, kvh_n)
        send(proj_msg.at[to], proj_in.at[kvh], send_sem.at[4], recv_sem.at[4], (ctx, to))

    proj_in[kvh] = proj_msg[kvh]
    drain(gains.at[0 : kvh_n - 1], recv_sem.at[3])
    drain(proj_in.at[0 : kvh_n - 1], recv_sem.at[4])
    carried = residual[...].astype(F32)
    for k in range(kvh_n):
        carried = carried + proj_in[k].astype(F32)
    carried = carried.astype(BF16)
    feats[core, 0] = carried

    far_hops = cuts[-1][0]
    outward = sorted(range(1, chips), key=lambda n: (chip_hops[n] < far_hops, n))
    for n in outward:
        to_ctx, to_x = chip_at[n]
        send(
            feats.at[core, 0],
            feats.at[core, chip_opposite[n]],
            send_sem.at[5],
            feat_sem.at[group_at[n]],
            (to_ctx, to_x * 2 + core),
        )

    width = 2 * LANES
    products = jnp.zeros((tokens, 2 * units), F32)
    squares = jnp.zeros((tokens, LANES), F32)

    def chip_columns(n):
        at_ctx, at_x = chip_at[n]
        return pl.ds(pl.multiple_of((at_ctx * x_n + at_x) * width, width), width)

    def relay(g):
        low, high = groups[g]
        drain(feats.at[core, low : high - 1 if g == 0 else high], feat_sem.at[g])
        block = feats.at[core, low:high]
        send(block, block, send_sem.at[6], relay_sem.at[g], partner)

    weight_copies[1].wait()
    weight_copies[2].wait()
    relay(0)
    for g, (low, high) in enumerate(groups):
        if g + 1 < len(groups):
            relay(g + 1)
        drain(feats.at[1 - core, low:high], relay_sem.at[g])
        pieces = []
        for n in range(low, high):
            at_ctx, at_x = chip_at[n]
            for c in range(2):
                piece = feats[c, n].astype(F32)
                squares = squares + piece * piece
                pieces.append((piece * gains[at_x * 2 + c, at_ctx]).astype(BF16))
        rows = jnp.concatenate(pieces, axis=1)
        matching = jnp.concatenate(
            [gate_up_w[:, chip_columns(n)] for n in range(low, high)], axis=1
        )
        products = products + dot_rows(rows, matching)
    mean_square = jnp.sum(squares, axis=1, keepdims=True) / (chips * 2 * LANES)
    products = products * lax.rsqrt(mean_square + EPSILON)
    gate = products[:, 0:units]
    up = products[:, units : 2 * units]
    hidden = (gate / (1.0 + jnp.exp(-gate)) * up).astype(BF16)

    weight_copies[3].wait()
    groups = groups[:1:-1] + [(0, groups[1][1])]

    def halves(g):
        low, high = groups[g]
        matching = jnp.concatenate([down_w[:, chip_columns(n)] for n in range(low, high)], axis=1)
        block = dot(hidden, matching)
        for n in range(low, high):
            for c in range(2):
                at = (n - low) * width + c * LANES
                piece = block[:, at : at + LANES]
                half_wide[c, n] = piece
                half_msg[c, n] = piece.astype(BF16)
        send(
            half_msg.at[1 - core, low:high],
            half_in.at[low:high],
            send_sem.at[7],
            half_sem.at[g],
            partner,
        )

    def spread(g):
        low, high = groups[g]
        drain(half_in.at[low:high], half_sem.at[g])
        pair_msg[low:high] = (half_wide[core, low:high] + half_in[low:high].astype(F32)).astype(
            BF16
        )
        for n in range(high - 1, max(low, 1) - 1, -1):
            to_ctx, to_x = chip_at[n]
            send(
                pair_msg.at[n],
                down_in.at[chip_opposite[n]],
                send_sem.at[8],
                recv_sem.at[5],
                (to_ctx, to_x * 2 + core),
            )

    for g in range(len(groups)):
        halves(g)
        if g >= 1:
            spread(g - 1)
    spread(len(groups) - 1)
    down_in[0] = pair_msg[0]
    drain(down_in.at[0 : chips - 1], recv_sem.at[5])
    final = carried.astype(F32) + jnp.sum(down_in[...].astype(F32), axis=0)
    result[...] = final.astype(BF16)

    drain(att_in.at[0 : ctx_n - 1], send_sem.at[0])
    drain(gains.at[0, 0 : ctx_n - 1], send_sem.at[1])
    drain(heads.at[0 : ctx_n - 1], send_sem.at[2])
    drain(gains.at[0 : kvh_n - 1], send_sem.at[3])
    drain(proj_in.at[0 : kvh_n - 1], send_sem.at[4])
    drain(down_in.at[0 : chips - 1], send_sem.at[5])
    drain(feats.at[0], send_sem.at[6])
    drain(half_in, send_sem.at[7])
    drain(down_in.at[0 : chips - 1], send_sem.at[8])


def per_device(ctx_n, kvh_n, planes, *arguments):
    (
        query,
        new_kv,
        kv_cache,
        lengths,
        residual,
        out_weight,
        norm_gain,
        gate_weight,
        up_weight,
        down_weight,
    ) = arguments
    steps, batch, query_width = query.shape
    heads = query_width // LANES
    assert heads == ctx_n and kv_cache.shape[2] == 1
    tokens = steps * batch
    chips = ctx_n * kvh_n // 2
    x_n = kvh_n // 2
    group_n = len(chip_groups(planes, ctx_n // planes, x_n))
    cache = kv_cache.reshape(2, batch, kv_cache.shape[3], LANES)
    units = gate_weight.shape[0]
    vmem = pl.BlockSpec(memory_space=pltpu.VMEM)
    far = pl.BlockSpec(memory_space=pl.ANY)
    dma = pltpu.SemaphoreType.DMA
    out = pl.pallas_call(
        functools.partial(layer_kernel, (ctx_n, kvh_n, planes, steps, batch)),
        out_shape=pltpu.VMEM((tokens, LANES), BF16),
        in_specs=[far] * 10,
        out_specs=vmem,
        scratch_shapes=[
            pltpu.VMEM(query.shape, BF16),
            pltpu.VMEM((2, tokens, LANES), BF16),
            pltpu.SMEM((batch,), jnp.int32),
            pltpu.VMEM((tokens, LANES), BF16),
            pltpu.VMEM((1, LANES), F32),
            pltpu.VMEM(cache.shape, BF16),
            pltpu.VMEM(out_weight.shape, BF16),
            pltpu.VMEM((2 * units, gate_weight.shape[1]), BF16),
            pltpu.VMEM(down_weight.shape, BF16),
            pltpu.VMEM((ctx_n * tokens, LANES), F32),
            pltpu.VMEM((ctx_n * tokens, LANES), F32),
            pltpu.VMEM((ctx_n * tokens, LANES), F32),
            pltpu.VMEM((ctx_n, 2 * tokens, LANES), BF16),
            pltpu.VMEM((ctx_n, 2 * tokens, LANES), BF16),
            pltpu.VMEM((ctx_n, tokens, LANES), BF16),
            pltpu.VMEM((kvh_n, tokens, LANES), BF16),
            pltpu.VMEM((kvh_n, tokens, LANES), BF16),
            pltpu.VMEM((kvh_n, ctx_n, 1, LANES), F32),
            pltpu.VMEM((2, chips, tokens, LANES), BF16),
            pltpu.VMEM((2, chips, tokens, LANES), F32),
            pltpu.VMEM((2, chips, tokens, LANES), BF16),
            pltpu.VMEM((chips, tokens, LANES), BF16),
            pltpu.VMEM((chips, tokens, LANES), BF16),
            pltpu.VMEM((chips, tokens, LANES), BF16),
            dma((5,)),
            dma((batch,)),
            dma((4,)),
            dma((9,)),
            dma((6,)),
            dma((2,)),
            dma((planes // 2 + ctx_n // planes // 2,)),
            dma((group_n,)),
            dma((group_n,)),
            dma((group_n,)),
        ],
        compiler_params=pltpu.CompilerParams(
            collective_id=0, has_side_effects=True, vmem_limit_bytes=56 * 2**20
        ),
        name="layer",
    )(
        query,
        new_kv.reshape(2, tokens, LANES),
        lengths,
        residual.reshape(tokens, LANES),
        norm_gain.reshape(1, LANES),
        cache,
        out_weight,
        gate_weight,
        up_weight,
        down_weight,
    )
    return out.reshape(steps, batch, LANES)


def solution(mesh):
    ctx_n, kvh_n = mesh.shape["ctx"], mesh.shape["kvh"]
    planes = 4 if ctx_n % 4 == 0 and ctx_n > 4 else 2
    return jax.shard_map(
        functools.partial(per_device, ctx_n, kvh_n, planes),
        mesh=mesh,
        in_specs=(
            P(None, None, "kvh"),
            P(None, None, None, "kvh"),
            P(None, None, "kvh", "ctx", None),
            P(),
            P(None, None, ("ctx", "kvh")),
            P("kvh", "ctx"),
            P(("ctx", "kvh")),
            P(("ctx", "kvh"), None),
            P(("ctx", "kvh"), None),
            P(("ctx", "kvh"), None),
        ),
        out_specs=P(None, None, ("ctx", "kvh")),
        check_vma=False,
    )
```

```python
import functools
import itertools
import math

import jax
import jax.numpy as jnp
from jax import lax
from jax.experimental import pallas as pl
from jax.experimental.pallas import tpu as pltpu
from jax.sharding import PartitionSpec as P

EPSILON = 1e-05
HIDE = -1e30
LANES = 128
MESH = pl.DeviceIdType.MESH
ROWS_BY_ROWS = (((1,), (1,)), ((), ()))
BF16 = jnp.bfloat16
F32 = jnp.float32


def dot(left, right):
    return jnp.dot(left, right, preferred_element_type=F32)


def dot_rows(left, right):
    return lax.dot_general(left, right, ROWS_BY_ROWS, preferred_element_type=F32)


def drain(ref, sem):
    pltpu.make_async_copy(ref, ref, sem).wait()


def chip_groups(*sizes):
    longest = sum(size // 2 for size in sizes)
    return [(0, 1), *((k, k) for k in range(2, longest - 1)), (longest - 1, longest)]


def layer_kernel(
    dims,
    query_hbm,
    draft_hbm,
    lengths_hbm,
    residual_hbm,
    gain_hbm,
    cache_hbm,
    out_hbm,
    gate_hbm,
    up_hbm,
    down_hbm,
    result,
    query,
    draft,
    lengths,
    residual,
    gain,
    cache,
    out_w,
    gate_up_w,
    down_w,
    gate_up_other,
    down_other,
    queries,
    numer,
    stats,
    att_msg,
    att_in,
    heads,
    proj_msg,
    proj_in,
    gains,
    feats,
    halves_out,
    halves_in,
    squares_out,
    squares_in,
    pair_msg,
    down_in,
    input_sem,
    cache_sem,
    weight_sem,
    send_sem,
    recv_sem,
    part_sem,
    head_sem,
    feat_sem,
):
    ctx_n, kvh_n, planes, steps, batch = dims
    x_n = kvh_n // 2
    z_n = ctx_n // planes
    chips = ctx_n * x_n
    tokens = steps * batch
    shard_len = cache.shape[2]
    units = down_w.shape[0]
    scale = 1.0 / math.sqrt(LANES)
    ctx = lax.axis_index("ctx")
    kvh = lax.axis_index("kvh")
    core = lax.rem(kvh, 2)
    x = lax.div(kvh, 2)
    chip = ctx * x_n + x
    plane = lax.div(ctx, z_n)
    place = lax.rem(ctx, z_n)
    partner = (ctx, kvh + 1 - 2 * core)

    def ring(at, size):
        return min(at, size - at)

    def ordered(*sizes):
        at = itertools.product(*(range(size) for size in sizes))
        hops = lambda o: sum(ring(a, size) for a, size in zip(o, sizes))
        offsets = sorted(at, key=lambda o: (hops(o), o))
        opposite = [
            offsets.index(tuple(-a % size for a, size in zip(o, sizes))) for o in offsets
        ]
        return offsets, opposite, [hops(o) for o in offsets]

    def ctx_of(dy, dz):
        return lax.rem(plane + dy, planes) * z_n + lax.rem(place + dz, z_n)

    def span(hops, low, high):
        inside = [n for n, h in enumerate(hops) if low <= h <= high]
        return inside[0], inside[-1] + 1

    offsets, opposite, hops = ordered(planes, z_n)
    ctx_at = [ctx_of(*o) for o in offsets]
    chip_offsets, chip_opposite, chip_hops = ordered(planes, z_n, x_n)
    chip_at = [(ctx_of(dy, dz), lax.rem(x + dx, x_n)) for dy, dz, dx in chip_offsets]
    cuts = chip_groups(planes, z_n, x_n)
    groups = [span(chip_hops, low, high) for low, high in cuts]
    group_at = [[low <= h <= high for low, high in cuts].index(True) for h in chip_hops]

    def send(src, dst, at_send, at_recv, device):
        pltpu.make_async_remote_copy(
            src_ref=src,
            dst_ref=dst,
            send_sem=at_send,
            recv_sem=at_recv,
            device_id=device,
            device_id_type=MESH,
        ).start()

    inputs = []
    for at, (src, dst) in enumerate(
        (
            (query_hbm, query),
            (draft_hbm, draft),
            (lengths_hbm, lengths),
            (residual_hbm, residual),
            (gain_hbm, gain),
        )
    ):
        copy = pltpu.make_async_copy(src, dst, input_sem.at[at])
        copy.start()
        inputs.append(copy)
    cache_copies = []
    for b in range(batch):
        copy = pltpu.make_async_copy(cache_hbm.at[:, b], cache.at[:, b], cache_sem.at[b])
        copy.start()
        cache_copies.append(copy)

    barrier = pltpu.get_barrier_semaphore()

    @pl.loop(1, ctx_n)
    def _(i):
        pl.semaphore_signal(
            barrier, inc=1, device_id=(lax.rem(ctx + i, ctx_n), kvh), device_id_type=MESH
        )

    @pl.loop(1, kvh_n)
    def _(i):
        pl.semaphore_signal(
            barrier, inc=1, device_id=(ctx, lax.rem(kvh + i, kvh_n)), device_id_type=MESH
        )

    for copy in inputs:
        copy.wait()

    for t in range(steps):
        row = query[t].astype(F32)
        for h in range(ctx_n):
            at = h * tokens + t * batch
            queries[at : at + batch, :] = row[:, h * LANES : (h + 1) * LANES]

    lane = lax.broadcasted_iota(jnp.int32, (ctx_n * steps, LANES), 1)
    position = ctx * shard_len + lax.broadcasted_iota(jnp.int32, (ctx_n * steps, shard_len), 1)
    draft_row = lax.broadcasted_iota(jnp.int32, (ctx_n * steps, tokens), 0)
    draft_col = lax.broadcasted_iota(jnp.int32, (ctx_n * steps, tokens), 1)
    draft_step = lax.div(draft_col, batch) + ctx * steps
    weight_copies = []
    for b in range(batch):
        cache_copies[b].wait()
        if b == batch - 1:
            for at, (src, dst) in enumerate(
                (
                    (out_hbm, out_w),
                    (gate_hbm, gate_up_w.at[0:units]),
                    (up_hbm, gate_up_w.at[units : 2 * units]),
                    (down_hbm, down_w),
                )
            ):
                copy = pltpu.make_async_copy(src, dst, weight_sem.at[at])
                copy.start()
                weight_copies.append(copy)
        mine = pl.ds(b, ctx_n * steps, stride=batch)
        q = queries[mine, :].astype(BF16)
        seen = position < lengths[b]
        scores = jnp.where(seen, dot_rows(q, cache[0, b]) * scale, HIDE)
        draft_seen = (draft_step <= lax.rem(draft_row, steps)) & (
            lax.rem(draft_col, batch) == b
        )
        draft_scores = jnp.where(draft_seen, dot_rows(q, draft[0]) * scale, HIDE)
        top = jnp.maximum(
            jnp.max(scores, axis=1, keepdims=True), jnp.max(draft_scores, axis=1, keepdims=True)
        )
        top = top.astype(BF16).astype(F32)
        weights = jnp.where(seen, jnp.exp(scores - top), 0.0)
        draft_weights = jnp.where(draft_seen, jnp.exp(draft_scores - top), 0.0)
        total = jnp.sum(weights, axis=1, keepdims=True) + jnp.sum(
            draft_weights, axis=1, keepdims=True
        )
        numer[mine, :] = dot(weights.astype(BF16), cache[1, b]) + dot(
            draft_weights.astype(BF16), draft[1]
        )
        stats[mine, :] = jnp.where(lane < 64, top, total)
    by_head = (ctx_n, tokens, LANES)
    att_msg[:, 0:tokens, :] = numer[...].reshape(by_head).astype(BF16)
    wide = stats[...].reshape(by_head)
    high = wide.astype(BF16).astype(F32)
    lanes3 = lax.broadcasted_iota(jnp.int32, by_head, 2)
    att_msg[:, tokens : 2 * tokens, :] = jnp.where(lanes3 < 96, high, wide - high).astype(BF16)

    pl.semaphore_wait(barrier, ctx_n + kvh_n - 2)

    for n in range(1, ctx_n):
        to = ctx_at[n]
        send(
            att_msg.at[to],
            att_in.at[opposite[n]],
            send_sem.at[0],
            part_sem.at[0 if hops[n] <= 2 else 1],
            (to, kvh),
        )
    att_in[0] = att_msg[ctx]

    gains[kvh, ctx] = gain[...]

    @pl.loop(1, ctx_n)
    def _(i):
        to = lax.rem(ctx + i, ctx_n)
        send(gains.at[kvh, ctx], gains.at[kvh, ctx], send_sem.at[1], recv_sem.at[1], (to, kvh))

    def side(n, which):
        at_ctx, at_x = chip_at[n]
        return pl.ds(pl.multiple_of(((at_ctx * x_n + at_x) * 2 + which) * LANES, LANES), LANES)

    def hand_over(src, dst, at_send, at_recv):
        for n in range(chips):
            send(
                src.at[:, side(n, 1 - core)],
                dst.at[:, n * LANES : (n + 1) * LANES],
                at_send,
                at_recv,
                partner,
            )

    hand_over(gate_hbm, gate_up_other.at[0:units], send_sem.at[9], recv_sem.at[6])

    def merged(low, high):
        parts = [att_in[i, tokens : 2 * tokens, :].astype(F32) for i in range(low, high)]
        tops = [jnp.broadcast_to(p[:, 0:1], (tokens, LANES)) for p in parts]
        highest = functools.reduce(jnp.maximum, tops)
        factors = [jnp.exp(t - highest) for t in tops]
        denominator = sum(f * (p[:, 64:65] + p[:, 96:97]) for f, p in zip(factors, parts))
        numerator = sum(
            f * att_in[low + i, 0:tokens, :].astype(F32) for i, f in enumerate(factors)
        )
        return highest, denominator, numerator

    low, high = span(hops, 0, 2)
    drain(att_in.at[0 : high - 1], part_sem.at[0])
    highest, denominator, numerator = merged(low, high)
    if high < ctx_n:
        drain(att_in.at[high:ctx_n], part_sem.at[1])
        highest2, denominator2, numerator2 = merged(high, ctx_n)
        top = jnp.maximum(highest, highest2)
        factor, factor2 = jnp.exp(highest - top), jnp.exp(highest2 - top)
        denominator = factor * denominator + factor2 * denominator2
        numerator = factor * numerator + factor2 * numerator2
    heads[0] = (numerator / denominator).astype(BF16)

    for n in range(1, ctx_n):
        send(
            heads.at[0],
            heads.at[opposite[n]],
            send_sem.at[2],
            head_sem.at[max(hops[n] - 1, 0)],
            (ctx_at[n], kvh),
        )

    hand_over(up_hbm, gate_up_other.at[units : 2 * units], send_sem.at[10], recv_sem.at[7])
    hand_over(down_hbm, down_other, send_sem.at[11], recv_sem.at[8])

    drain(gains.at[0, 0 : ctx_n - 1], recv_sem.at[1])

    @pl.loop(1, kvh_n)
    def _(i):
        to = lax.rem(kvh + i, kvh_n)
        send(gains.at[kvh], gains.at[kvh], send_sem.at[3], recv_sem.at[3], (ctx, to))

    weight_copies[0].wait()
    projected = jnp.zeros((tokens, kvh_n * LANES), F32)
    for at, (first, last) in enumerate(((0, 1), (2, 2), (3, hops[-1]))):
        if first > last:
            continue
        low, high = span(hops, first, last)
        for k in range(max(first, 1), last + 1):
            start, end = span(hops, k, k)
            drain(heads.at[start:end], head_sem.at[k - 1])
        attended = jnp.concatenate([heads[n] for n in range(low, high)], axis=1)
        rows = jnp.concatenate(
            [
                out_w[pl.ds(pl.multiple_of(ctx_at[n] * LANES, LANES), LANES), :]
                for n in range(low, high)
            ],
            axis=0,
        )
        projected = projected + dot(attended, rows)
    for k in range(kvh_n):
        proj_msg[k] = projected[:, k * LANES : (k + 1) * LANES].astype(BF16)

    @pl.loop(1, kvh_n)
    def _(i):
        to = lax.rem(kvh + i, kvh_n)
        send(proj_msg.at[to], proj_in.at[kvh], send_sem.at[4], recv_sem.at[4], (ctx, to))

    proj_in[kvh] = proj_msg[kvh]
    drain(gains.at[0 : kvh_n - 1], recv_sem.at[3])
    drain(proj_in.at[0 : kvh_n - 1], recv_sem.at[4])
    carried = residual[...].astype(F32)
    for k in range(kvh_n):
        carried = carried + proj_in[k].astype(F32)
    carried = carried.astype(BF16)
    feats[0] = carried

    far_hops = cuts[-1][0]
    outward = sorted(range(1, chips), key=lambda n: (chip_hops[n] < far_hops, n))
    for n in outward:
        to_ctx, to_x = chip_at[n]
        send(
            feats.at[0],
            feats.at[chip_opposite[n]],
            send_sem.at[5],
            feat_sem.at[group_at[n]],
            (to_ctx, to_x * 2 + core),
        )

    weight_copies[1].wait()
    weight_copies[2].wait()
    drain(gate_up_other.at[0:units], recv_sem.at[6])
    drain(gate_up_other.at[units : 2 * units], recv_sem.at[7])
    products = jnp.zeros((tokens, 2 * units), F32)
    products_other = jnp.zeros((tokens, 2 * units), F32)
    squares = jnp.zeros((tokens, LANES), F32)
    for g, (low, high) in enumerate(groups):
        drain(feats.at[low : high - 1 if g == 0 else high], feat_sem.at[g])
        pieces = []
        for n in range(low, high):
            at_ctx, at_x = chip_at[n]
            piece = feats[n].astype(F32)
            squares = squares + piece * piece
            pieces.append((piece * gains[at_x * 2 + core, at_ctx]).astype(BF16))
        rows = jnp.concatenate(pieces, axis=1)
        matching = jnp.concatenate([gate_up_w[:, side(n, core)] for n in range(low, high)], axis=1)
        products = products + dot_rows(rows, matching)
        matching = gate_up_other[:, low * LANES : high * LANES]
        products_other = products_other + dot_rows(rows, matching)
    halves_out[0] = products
    halves_out[1] = products_other
    squares_out[...] = squares
    send(halves_out, halves_in, send_sem.at[6], recv_sem.at[9], partner)
    send(squares_out, squares_in, send_sem.at[7], recv_sem.at[10], partner)
    drain(halves_in, recv_sem.at[9])
    drain(squares_in, recv_sem.at[10])
    squares = squares + squares_in[...]
    mean_square = jnp.sum(squares, axis=1, keepdims=True) / (chips * 2 * LANES)
    inverse = lax.rsqrt(mean_square + EPSILON)

    def activated(total):
        gate = total[:, 0:units] * inverse
        up = total[:, units : 2 * units] * inverse
        return (gate / (1.0 + jnp.exp(-gate)) * up).astype(BF16)

    hidden = activated(products + halves_in[1])
    hidden_other = activated(products_other + halves_in[0])

    weight_copies[3].wait()
    drain(down_other, recv_sem.at[8])
    for low, high in groups[:1:-1] + [(0, groups[1][1])]:
        matching = jnp.concatenate([down_w[:, side(n, core)] for n in range(low, high)], axis=1)
        block = dot(hidden, matching)
        block = block + dot(hidden_other, down_other[:, low * LANES : high * LANES])
        for n in range(high - 1, low - 1, -1):
            pair_msg[n] = block[:, (n - low) * LANES : (n - low + 1) * LANES].astype(BF16)
        for n in range(high - 1, max(low, 1) - 1, -1):
            to_ctx, to_x = chip_at[n]
            send(
                pair_msg.at[n],
                down_in.at[chip_opposite[n]],
                send_sem.at[8],
                recv_sem.at[5],
                (to_ctx, to_x * 2 + core),
            )
    down_in[0] = pair_msg[0]
    drain(down_in.at[0 : chips - 1], recv_sem.at[5])
    final = carried.astype(F32) + jnp.sum(down_in[...].astype(F32), axis=0)
    result[...] = final.astype(BF16)

    drain(att_in.at[0 : ctx_n - 1], send_sem.at[0])
    drain(gains.at[0, 0 : ctx_n - 1], send_sem.at[1])
    drain(heads.at[0 : ctx_n - 1], send_sem.at[2])
    drain(gains.at[0 : kvh_n - 1], send_sem.at[3])
    drain(proj_in.at[0 : kvh_n - 1], send_sem.at[4])
    drain(down_in.at[0 : chips - 1], send_sem.at[5])
    drain(halves_in, send_sem.at[6])
    drain(squares_in, send_sem.at[7])
    drain(down_in.at[0 : chips - 1], send_sem.at[8])
    drain(down_other, send_sem.at[9])
    drain(down_other, send_sem.at[10])
    drain(down_other, send_sem.at[11])


def per_device(ctx_n, kvh_n, planes, *arguments):
    (
        query,
        new_kv,
        kv_cache,
        lengths,
        residual,
        out_weight,
        norm_gain,
        gate_weight,
        up_weight,
        down_weight,
    ) = arguments
    steps, batch, query_width = query.shape
    heads = query_width // LANES
    assert heads == ctx_n and kv_cache.shape[2] == 1
    tokens = steps * batch
    chips = ctx_n * kvh_n // 2
    x_n = kvh_n // 2
    group_n = len(chip_groups(planes, ctx_n // planes, x_n))
    cache = kv_cache.reshape(2, batch, kv_cache.shape[3], LANES)
    units = gate_weight.shape[0]
    vmem = pl.BlockSpec(memory_space=pltpu.VMEM)
    far = pl.BlockSpec(memory_space=pl.ANY)
    dma = pltpu.SemaphoreType.DMA
    out = pl.pallas_call(
        functools.partial(layer_kernel, (ctx_n, kvh_n, planes, steps, batch)),
        out_shape=pltpu.VMEM((tokens, LANES), BF16),
        in_specs=[far] * 10,
        out_specs=vmem,
        scratch_shapes=[
            pltpu.VMEM(query.shape, BF16),
            pltpu.VMEM((2, tokens, LANES), BF16),
            pltpu.SMEM((batch,), jnp.int32),
            pltpu.VMEM((tokens, LANES), BF16),
            pltpu.VMEM((1, LANES), F32),
            pltpu.VMEM(cache.shape, BF16),
            pltpu.VMEM(out_weight.shape, BF16),
            pltpu.VMEM((2 * units, gate_weight.shape[1]), BF16),
            pltpu.VMEM(down_weight.shape, BF16),
            pltpu.VMEM((2 * units, chips * LANES), BF16),
            pltpu.VMEM((units, chips * LANES), BF16),
            pltpu.VMEM((ctx_n * tokens, LANES), F32),
            pltpu.VMEM((ctx_n * tokens, LANES), F32),
            pltpu.VMEM((ctx_n * tokens, LANES), F32),
            pltpu.VMEM((ctx_n, 2 * tokens, LANES), BF16),
            pltpu.VMEM((ctx_n, 2 * tokens, LANES), BF16),
            pltpu.VMEM((ctx_n, tokens, LANES), BF16),
            pltpu.VMEM((kvh_n, tokens, LANES), BF16),
            pltpu.VMEM((kvh_n, tokens, LANES), BF16),
            pltpu.VMEM((kvh_n, ctx_n, 1, LANES), F32),
            pltpu.VMEM((chips, tokens, LANES), BF16),
            pltpu.VMEM((2, tokens, 2 * units), F32),
            pltpu.VMEM((2, tokens, 2 * units), F32),
            pltpu.VMEM((tokens, LANES), F32),
            pltpu.VMEM((tokens, LANES), F32),
            pltpu.VMEM((chips, tokens, LANES), BF16),
            pltpu.VMEM((chips, tokens, LANES), BF16),
            dma((5,)),
            dma((batch,)),
            dma((4,)),
            dma((12,)),
            dma((11,)),
            dma((2,)),
            dma((planes // 2 + ctx_n // planes // 2,)),
            dma((group_n,)),
        ],
        compiler_params=pltpu.CompilerParams(
            collective_id=0, has_side_effects=True, vmem_limit_bytes=56 * 2**20
        ),
        name="layer",
    )(
        query,
        new_kv.reshape(2, tokens, LANES),
        lengths,
        residual.reshape(tokens, LANES),
        norm_gain.reshape(1, LANES),
        cache,
        out_weight,
        gate_weight,
        up_weight,
        down_weight,
    )
    return out.reshape(steps, batch, LANES)


def solution(mesh):
    ctx_n, kvh_n = mesh.shape["ctx"], mesh.shape["kvh"]
    planes = 4 if ctx_n % 4 == 0 and ctx_n > 4 else 2
    return jax.shard_map(
        functools.partial(per_device, ctx_n, kvh_n, planes),
        mesh=mesh,
        in_specs=(
            P(None, None, "kvh"),
            P(None, None, None, "kvh"),
            P(None, None, "kvh", "ctx", None),
            P(),
            P(None, None, ("ctx", "kvh")),
            P("kvh", "ctx"),
            P(("ctx", "kvh")),
            P(("ctx", "kvh"), None),
            P(("ctx", "kvh"), None),
            P(("ctx", "kvh"), None),
        ),
        out_specs=P(None, None, ("ctx", "kvh")),
        check_vma=False,
    )
```

```python
import functools
import itertools
import math

import jax
import jax.numpy as jnp
from jax import lax
from jax.experimental import pallas as pl
from jax.experimental.pallas import tpu as pltpu
from jax.sharding import PartitionSpec as P

EPSILON = 1e-05
HIDE = -1e30
LANES = 128
MESH = pl.DeviceIdType.MESH
ROWS_BY_ROWS = (((1,), (1,)), ((), ()))
BF16 = jnp.bfloat16
F32 = jnp.float32


def dot(left, right):
    return jnp.dot(left, right, preferred_element_type=F32)


def dot_rows(left, right):
    return lax.dot_general(left, right, ROWS_BY_ROWS, preferred_element_type=F32)


def drain(ref, sem):
    pltpu.make_async_copy(ref, ref, sem).wait()


def chip_groups(*sizes):
    longest = sum(size // 2 for size in sizes)
    return [(0, 1), *((k, k) for k in range(2, longest - 1)), (longest - 1, longest)]


def layer_kernel(
    dims,
    query_hbm,
    draft_hbm,
    lengths_hbm,
    residual_hbm,
    gain_hbm,
    cache_hbm,
    out_hbm,
    gate_hbm,
    up_hbm,
    down_hbm,
    result,
    query,
    draft,
    lengths,
    residual,
    gain,
    cache,
    out_w,
    gate_up_w,
    down_w,
    gate_up_other,
    down_other,
    queries,
    numer,
    stats,
    att_msg,
    att_in,
    heads,
    proj_msg,
    proj_in,
    gains,
    feats,
    halves_out,
    halves_in,
    squares_out,
    squares_in,
    pair_msg,
    down_in,
    input_sem,
    cache_sem,
    weight_sem,
    send_sem,
    recv_sem,
    part_sem,
    head_sem,
    feat_sem,
):
    ctx_n, kvh_n, planes, steps, batch = dims
    x_n = kvh_n // 2
    z_n = ctx_n // planes
    chips = ctx_n * x_n
    tokens = steps * batch
    shard_len = cache.shape[2]
    units = down_w.shape[0]
    scale = 1.0 / math.sqrt(LANES)
    ctx = lax.axis_index("ctx")
    kvh = lax.axis_index("kvh")
    core = lax.rem(kvh, 2)
    x = lax.div(kvh, 2)
    chip = ctx * x_n + x
    plane = lax.div(ctx, z_n)
    place = lax.rem(ctx, z_n)
    partner = (ctx, kvh + 1 - 2 * core)

    def ring(at, size):
        return min(at, size - at)

    def ordered(*sizes):
        at = itertools.product(*(range(size) for size in sizes))
        hops = lambda o: sum(ring(a, size) for a, size in zip(o, sizes))
        offsets = sorted(at, key=lambda o: (hops(o), o))
        opposite = [
            offsets.index(tuple(-a % size for a, size in zip(o, sizes))) for o in offsets
        ]
        return offsets, opposite, [hops(o) for o in offsets]

    def ctx_of(dy, dz):
        return lax.rem(plane + dy, planes) * z_n + lax.rem(place + dz, z_n)

    def span(hops, low, high):
        inside = [n for n, h in enumerate(hops) if low <= h <= high]
        return inside[0], inside[-1] + 1

    offsets, opposite, hops = ordered(planes, z_n)
    ctx_at = [ctx_of(*o) for o in offsets]
    chip_offsets, chip_opposite, chip_hops = ordered(planes, z_n, x_n)
    chip_at = [(ctx_of(dy, dz), lax.rem(x + dx, x_n)) for dy, dz, dx in chip_offsets]
    cuts = chip_groups(planes, z_n, x_n)
    groups = [span(chip_hops, low, high) for low, high in cuts]
    group_at = [[low <= h <= high for low, high in cuts].index(True) for h in chip_hops]

    def send(src, dst, at_send, at_recv, device):
        pltpu.make_async_remote_copy(
            src_ref=src,
            dst_ref=dst,
            send_sem=at_send,
            recv_sem=at_recv,
            device_id=device,
            device_id_type=MESH,
        ).start()

    inputs = []
    for at, (src, dst) in enumerate(
        (
            (query_hbm, query),
            (draft_hbm, draft),
            (lengths_hbm, lengths),
            (residual_hbm, residual),
            (gain_hbm, gain),
        )
    ):
        copy = pltpu.make_async_copy(src, dst, input_sem.at[at])
        copy.start()
        inputs.append(copy)
    cache_copies = []
    for b in range(batch):
        copy = pltpu.make_async_copy(cache_hbm.at[:, b], cache.at[:, b], cache_sem.at[b])
        copy.start()
        cache_copies.append(copy)

    barrier = pltpu.get_barrier_semaphore()

    @pl.loop(1, ctx_n)
    def _(i):
        pl.semaphore_signal(
            barrier, inc=1, device_id=(lax.rem(ctx + i, ctx_n), kvh), device_id_type=MESH
        )

    @pl.loop(1, kvh_n)
    def _(i):
        pl.semaphore_signal(
            barrier, inc=1, device_id=(ctx, lax.rem(kvh + i, kvh_n)), device_id_type=MESH
        )

    for copy in inputs:
        copy.wait()

    for t in range(steps):
        row = query[t].astype(F32)
        for h in range(ctx_n):
            at = h * tokens + t * batch
            queries[at : at + batch, :] = row[:, h * LANES : (h + 1) * LANES]

    lane = lax.broadcasted_iota(jnp.int32, (ctx_n * steps, LANES), 1)
    position = ctx * shard_len + lax.broadcasted_iota(jnp.int32, (ctx_n * steps, shard_len), 1)
    draft_row = lax.broadcasted_iota(jnp.int32, (ctx_n * steps, tokens), 0)
    draft_col = lax.broadcasted_iota(jnp.int32, (ctx_n * steps, tokens), 1)
    draft_step = lax.div(draft_col, batch) + ctx * steps
    weight_copies = []
    for b in range(batch):
        cache_copies[b].wait()
        if b == batch - 1:
            for at, (src, dst) in enumerate(
                (
                    (out_hbm, out_w),
                    (gate_hbm, gate_up_w.at[0:units]),
                    (up_hbm, gate_up_w.at[units : 2 * units]),
                    (down_hbm, down_w),
                )
            ):
                copy = pltpu.make_async_copy(src, dst, weight_sem.at[at])
                copy.start()
                weight_copies.append(copy)
        mine = pl.ds(b, ctx_n * steps, stride=batch)
        q = queries[mine, :].astype(BF16)
        seen = position < lengths[b]
        scores = jnp.where(seen, dot_rows(q, cache[0, b]) * scale, HIDE)
        draft_seen = (draft_step <= lax.rem(draft_row, steps)) & (
            lax.rem(draft_col, batch) == b
        )
        draft_scores = jnp.where(draft_seen, dot_rows(q, draft[0]) * scale, HIDE)
        top = jnp.maximum(
            jnp.max(scores, axis=1, keepdims=True), jnp.max(draft_scores, axis=1, keepdims=True)
        )
        top = top.astype(BF16).astype(F32)
        weights = jnp.where(seen, jnp.exp(scores - top), 0.0)
        draft_weights = jnp.where(draft_seen, jnp.exp(draft_scores - top), 0.0)
        total = jnp.sum(weights, axis=1, keepdims=True) + jnp.sum(
            draft_weights, axis=1, keepdims=True
        )
        numer[mine, :] = dot(weights.astype(BF16), cache[1, b]) + dot(
            draft_weights.astype(BF16), draft[1]
        )
        stats[mine, :] = jnp.where(lane < 64, top, total)
    by_head = (ctx_n, tokens, LANES)
    att_msg[:, 0:tokens, :] = numer[...].reshape(by_head).astype(BF16)
    wide = stats[...].reshape(by_head)
    high = wide.astype(BF16).astype(F32)
    lanes3 = lax.broadcasted_iota(jnp.int32, by_head, 2)
    att_msg[:, tokens : 2 * tokens, :] = jnp.where(lanes3 < 96, high, wide - high).astype(BF16)

    pl.semaphore_wait(barrier, ctx_n + kvh_n - 2)

    for n in range(1, ctx_n):
        to = ctx_at[n]
        send(
            att_msg.at[to],
            att_in.at[opposite[n]],
            send_sem.at[0],
            part_sem.at[0 if hops[n] <= 2 else 1],
            (to, kvh),
        )
    att_in[0] = att_msg[ctx]

    gains[kvh, ctx] = gain[...]

    @pl.loop(1, ctx_n)
    def _(i):
        to = lax.rem(ctx + i, ctx_n)
        send(gains.at[kvh, ctx], gains.at[kvh, ctx], send_sem.at[1], recv_sem.at[1], (to, kvh))

    def side(n, which):
        at_ctx, at_x = chip_at[n]
        return pl.ds(pl.multiple_of(((at_ctx * x_n + at_x) * 2 + which) * LANES, LANES), LANES)

    def hand_over(src, dst, at_send, at_recv):
        for n in range(chips):
            send(
                src.at[:, side(n, 1 - core)],
                dst.at[:, n * LANES : (n + 1) * LANES],
                at_send,
                at_recv,
                partner,
            )

    hand_over(gate_hbm, gate_up_other.at[0:units], send_sem.at[9], recv_sem.at[6])

    def merged(low, high):
        parts = [att_in[i, tokens : 2 * tokens, :].astype(F32) for i in range(low, high)]
        tops = [jnp.broadcast_to(p[:, 0:1], (tokens, LANES)) for p in parts]
        highest = functools.reduce(jnp.maximum, tops)
        factors = [jnp.exp(t - highest) for t in tops]
        denominator = sum(f * (p[:, 64:65] + p[:, 96:97]) for f, p in zip(factors, parts))
        numerator = sum(
            f * att_in[low + i, 0:tokens, :].astype(F32) for i, f in enumerate(factors)
        )
        return highest, denominator, numerator

    low, high = span(hops, 0, 2)
    drain(att_in.at[0 : high - 1], part_sem.at[0])
    highest, denominator, numerator = merged(low, high)
    if high < ctx_n:
        drain(att_in.at[high:ctx_n], part_sem.at[1])
        highest2, denominator2, numerator2 = merged(high, ctx_n)
        top = jnp.maximum(highest, highest2)
        factor, factor2 = jnp.exp(highest - top), jnp.exp(highest2 - top)
        denominator = factor * denominator + factor2 * denominator2
        numerator = factor * numerator + factor2 * numerator2
    heads[0] = (numerator / denominator).astype(BF16)

    for n in range(1, ctx_n):
        send(
            heads.at[0],
            heads.at[opposite[n]],
            send_sem.at[2],
            head_sem.at[max(hops[n] - 1, 0)],
            (ctx_at[n], kvh),
        )

    hand_over(up_hbm, gate_up_other.at[units : 2 * units], send_sem.at[10], recv_sem.at[7])

    drain(gains.at[0, 0 : ctx_n - 1], recv_sem.at[1])

    @pl.loop(1, kvh_n)
    def _(i):
        to = lax.rem(kvh + i, kvh_n)
        send(gains.at[kvh], gains.at[kvh], send_sem.at[3], recv_sem.at[3], (ctx, to))

    weight_copies[0].wait()
    projected = jnp.zeros((tokens, kvh_n * LANES), F32)
    for at, (first, last) in enumerate(((0, 1), (2, 2), (3, hops[-1]))):
        if first > last:
            continue
        low, high = span(hops, first, last)
        for k in range(max(first, 1), last + 1):
            start, end = span(hops, k, k)
            drain(heads.at[start:end], head_sem.at[k - 1])
        attended = jnp.concatenate([heads[n] for n in range(low, high)], axis=1)
        rows = jnp.concatenate(
            [
                out_w[pl.ds(pl.multiple_of(ctx_at[n] * LANES, LANES), LANES), :]
                for n in range(low, high)
            ],
            axis=0,
        )
        projected = projected + dot(attended, rows)
    for k in range(kvh_n):
        proj_msg[k] = projected[:, k * LANES : (k + 1) * LANES].astype(BF16)

    @pl.loop(1, kvh_n)
    def _(i):
        to = lax.rem(kvh + i, kvh_n)
        send(proj_msg.at[to], proj_in.at[kvh], send_sem.at[4], recv_sem.at[4], (ctx, to))

    proj_in[kvh] = proj_msg[kvh]
    hand_over(down_hbm, down_other, send_sem.at[11], recv_sem.at[8])
    drain(gains.at[0 : kvh_n - 1], recv_sem.at[3])
    drain(proj_in.at[0 : kvh_n - 1], recv_sem.at[4])
    carried = residual[...].astype(F32)
    for k in range(kvh_n):
        carried = carried + proj_in[k].astype(F32)
    carried = carried.astype(BF16)
    feats[0] = carried

    for n in range(1, chips):
        to_ctx, to_x = chip_at[n]
        send(
            feats.at[0],
            feats.at[chip_opposite[n]],
            send_sem.at[5],
            feat_sem.at[group_at[n]],
            (to_ctx, to_x * 2 + core),
        )

    weight_copies[1].wait()
    weight_copies[2].wait()
    drain(gate_up_other.at[0:units], recv_sem.at[6])
    drain(gate_up_other.at[units : 2 * units], recv_sem.at[7])
    products = jnp.zeros((tokens, 2 * units), F32)
    products_other = jnp.zeros((tokens, 2 * units), F32)
    squares = jnp.zeros((tokens, LANES), F32)
    for g, (low, high) in enumerate(groups):
        drain(feats.at[low : high - 1 if g == 0 else high], feat_sem.at[g])
        pieces = []
        for n in range(low, high):
            at_ctx, at_x = chip_at[n]
            piece = feats[n].astype(F32)
            squares = squares + piece * piece
            pieces.append((piece * gains[at_x * 2 + core, at_ctx]).astype(BF16))
        rows = jnp.concatenate(pieces, axis=1)
        matching = jnp.concatenate([gate_up_w[:, side(n, core)] for n in range(low, high)], axis=1)
        products = products + dot_rows(rows, matching)
        matching = gate_up_other[:, low * LANES : high * LANES]
        products_other = products_other + dot_rows(rows, matching)
    halves_out[0] = products
    halves_out[1] = products_other
    squares_out[...] = squares
    send(halves_out, halves_in, send_sem.at[6], recv_sem.at[9], partner)
    send(squares_out, squares_in, send_sem.at[7], recv_sem.at[10], partner)
    drain(halves_in, recv_sem.at[9])
    drain(squares_in, recv_sem.at[10])
    squares = squares + squares_in[...]
    mean_square = jnp.sum(squares, axis=1, keepdims=True) / (chips * 2 * LANES)
    inverse = lax.rsqrt(mean_square + EPSILON)

    def activated(total):
        gate = total[:, 0:units] * inverse
        up = total[:, units : 2 * units] * inverse
        return (gate / (1.0 + jnp.exp(-gate)) * up).astype(BF16)

    hidden = activated(products + halves_in[1])
    hidden_other = activated(products_other + halves_in[0])

    weight_copies[3].wait()
    drain(down_other, recv_sem.at[8])
    for low, high in groups[:1:-1] + [(0, groups[1][1])]:
        matching = jnp.concatenate([down_w[:, side(n, core)] for n in range(low, high)], axis=1)
        block = dot(hidden, matching)
        block = block + dot(hidden_other, down_other[:, low * LANES : high * LANES])
        for n in range(high - 1, low - 1, -1):
            pair_msg[n] = block[:, (n - low) * LANES : (n - low + 1) * LANES].astype(BF16)
        for n in range(high - 1, max(low, 1) - 1, -1):
            to_ctx, to_x = chip_at[n]
            send(
                pair_msg.at[n],
                down_in.at[chip_opposite[n]],
                send_sem.at[8],
                recv_sem.at[5],
                (to_ctx, to_x * 2 + core),
            )
    down_in[0] = pair_msg[0]
    drain(down_in.at[0 : chips - 1], recv_sem.at[5])
    final = carried.astype(F32) + jnp.sum(down_in[...].astype(F32), axis=0)
    result[...] = final.astype(BF16)

    drain(att_in.at[0 : ctx_n - 1], send_sem.at[0])
    drain(gains.at[0, 0 : ctx_n - 1], send_sem.at[1])
    drain(heads.at[0 : ctx_n - 1], send_sem.at[2])
    drain(gains.at[0 : kvh_n - 1], send_sem.at[3])
    drain(proj_in.at[0 : kvh_n - 1], send_sem.at[4])
    drain(down_in.at[0 : chips - 1], send_sem.at[5])
    drain(halves_in, send_sem.at[6])
    drain(squares_in, send_sem.at[7])
    drain(down_in.at[0 : chips - 1], send_sem.at[8])
    drain(down_other, send_sem.at[9])
    drain(down_other, send_sem.at[10])
    drain(down_other, send_sem.at[11])


def per_device(ctx_n, kvh_n, planes, *arguments):
    (
        query,
        new_kv,
        kv_cache,
        lengths,
        residual,
        out_weight,
        norm_gain,
        gate_weight,
        up_weight,
        down_weight,
    ) = arguments
    steps, batch, query_width = query.shape
    heads = query_width // LANES
    assert heads == ctx_n and kv_cache.shape[2] == 1
    tokens = steps * batch
    chips = ctx_n * kvh_n // 2
    x_n = kvh_n // 2
    group_n = len(chip_groups(planes, ctx_n // planes, x_n))
    cache = kv_cache.reshape(2, batch, kv_cache.shape[3], LANES)
    units = gate_weight.shape[0]
    vmem = pl.BlockSpec(memory_space=pltpu.VMEM)
    far = pl.BlockSpec(memory_space=pl.ANY)
    dma = pltpu.SemaphoreType.DMA
    out = pl.pallas_call(
        functools.partial(layer_kernel, (ctx_n, kvh_n, planes, steps, batch)),
        out_shape=pltpu.VMEM((tokens, LANES), BF16),
        in_specs=[far] * 10,
        out_specs=vmem,
        scratch_shapes=[
            pltpu.VMEM(query.shape, BF16),
            pltpu.VMEM((2, tokens, LANES), BF16),
            pltpu.SMEM((batch,), jnp.int32),
            pltpu.VMEM((tokens, LANES), BF16),
            pltpu.VMEM((1, LANES), F32),
            pltpu.VMEM(cache.shape, BF16),
            pltpu.VMEM(out_weight.shape, BF16),
            pltpu.VMEM((2 * units, gate_weight.shape[1]), BF16),
            pltpu.VMEM(down_weight.shape, BF16),
            pltpu.VMEM((2 * units, chips * LANES), BF16),
            pltpu.VMEM((units, chips * LANES), BF16),
            pltpu.VMEM((ctx_n * tokens, LANES), F32),
            pltpu.VMEM((ctx_n * tokens, LANES), F32),
            pltpu.VMEM((ctx_n * tokens, LANES), F32),
            pltpu.VMEM((ctx_n, 2 * tokens, LANES), BF16),
            pltpu.VMEM((ctx_n, 2 * tokens, LANES), BF16),
            pltpu.VMEM((ctx_n, tokens, LANES), BF16),
            pltpu.VMEM((kvh_n, tokens, LANES), BF16),
            pltpu.VMEM((kvh_n, tokens, LANES), BF16),
            pltpu.VMEM((kvh_n, ctx_n, 1, LANES), F32),
            pltpu.VMEM((chips, tokens, LANES), BF16),
            pltpu.VMEM((2, tokens, 2 * units), F32),
            pltpu.VMEM((2, tokens, 2 * units), F32),
            pltpu.VMEM((tokens, LANES), F32),
            pltpu.VMEM((tokens, LANES), F32),
            pltpu.VMEM((chips, tokens, LANES), BF16),
            pltpu.VMEM((chips, tokens, LANES), BF16),
            dma((5,)),
            dma((batch,)),
            dma((4,)),
            dma((12,)),
            dma((11,)),
            dma((2,)),
            dma((planes // 2 + ctx_n // planes // 2,)),
            dma((group_n,)),
        ],
        compiler_params=pltpu.CompilerParams(
            collective_id=0, has_side_effects=True, vmem_limit_bytes=56 * 2**20
        ),
        name="layer",
    )(
        query,
        new_kv.reshape(2, tokens, LANES),
        lengths,
        residual.reshape(tokens, LANES),
        norm_gain.reshape(1, LANES),
        cache,
        out_weight,
        gate_weight,
        up_weight,
        down_weight,
    )
    return out.reshape(steps, batch, LANES)


def solution(mesh):
    ctx_n, kvh_n = mesh.shape["ctx"], mesh.shape["kvh"]
    planes = 4 if ctx_n % 4 == 0 and ctx_n > 4 else 2
    return jax.shard_map(
        functools.partial(per_device, ctx_n, kvh_n, planes),
        mesh=mesh,
        in_specs=(
            P(None, None, "kvh"),
            P(None, None, None, "kvh"),
            P(None, None, "kvh", "ctx", None),
            P(),
            P(None, None, ("ctx", "kvh")),
            P("kvh", "ctx"),
            P(("ctx", "kvh")),
            P(("ctx", "kvh"), None),
            P(("ctx", "kvh"), None),
            P(("ctx", "kvh"), None),
        ),
        out_specs=P(None, None, ("ctx", "kvh")),
        check_vma=False,
    )
```

```python
import functools
import itertools
import math

import jax
import jax.numpy as jnp
from jax import lax
from jax.experimental import pallas as pl
from jax.experimental.pallas import tpu as pltpu
from jax.sharding import PartitionSpec as P

EPSILON = 1e-05
HIDE = -1e30
LANES = 128
MESH = pl.DeviceIdType.MESH
ROWS_BY_ROWS = (((1,), (1,)), ((), ()))
BF16 = jnp.bfloat16
F32 = jnp.float32


def dot(left, right):
    return jnp.dot(left, right, preferred_element_type=F32)


def dot_rows(left, right):
    return lax.dot_general(left, right, ROWS_BY_ROWS, preferred_element_type=F32)


def drain(ref, sem):
    pltpu.make_async_copy(ref, ref, sem).wait()


def chip_groups(*sizes):
    longest = sum(size // 2 for size in sizes)
    return [(0, 1), *((k, k) for k in range(2, longest - 1)), (longest - 1, longest)]


def layer_kernel(
    dims,
    query_hbm,
    draft_hbm,
    lengths_hbm,
    residual_hbm,
    gain_hbm,
    cache_hbm,
    out_hbm,
    gate_hbm,
    up_hbm,
    down_hbm,
    result,
    query,
    draft,
    lengths,
    residual,
    gain,
    cache,
    out_w,
    gate_up_w,
    down_w,
    gate_up_other,
    down_other,
    queries,
    numer,
    stats,
    att_msg,
    att_in,
    heads,
    proj_msg,
    proj_in,
    gains,
    feats,
    halves_out,
    halves_in,
    squares_out,
    squares_in,
    pair_msg,
    down_in,
    input_sem,
    cache_sem,
    weight_sem,
    send_sem,
    recv_sem,
    part_sem,
    head_sem,
    feat_sem,
):
    ctx_n, kvh_n, planes, steps, batch = dims
    x_n = kvh_n // 2
    z_n = ctx_n // planes
    chips = ctx_n * x_n
    tokens = steps * batch
    shard_len = cache.shape[2]
    units = down_w.shape[0]
    scale = 1.0 / math.sqrt(LANES)
    ctx = lax.axis_index("ctx")
    kvh = lax.axis_index("kvh")
    core = lax.rem(kvh, 2)
    x = lax.div(kvh, 2)
    chip = ctx * x_n + x
    plane = lax.div(ctx, z_n)
    place = lax.rem(ctx, z_n)
    partner = (ctx, kvh + 1 - 2 * core)

    def ring(at, size):
        return min(at, size - at)

    def ordered(*sizes):
        at = itertools.product(*(range(size) for size in sizes))
        hops = lambda o: sum(ring(a, size) for a, size in zip(o, sizes))
        offsets = sorted(at, key=lambda o: (hops(o), o))
        opposite = [
            offsets.index(tuple(-a % size for a, size in zip(o, sizes))) for o in offsets
        ]
        return offsets, opposite, [hops(o) for o in offsets]

    def ctx_of(dy, dz):
        return lax.rem(plane + dy, planes) * z_n + lax.rem(place + dz, z_n)

    def span(hops, low, high):
        inside = [n for n, h in enumerate(hops) if low <= h <= high]
        return inside[0], inside[-1] + 1

    offsets, opposite, hops = ordered(planes, z_n)
    ctx_at = [ctx_of(*o) for o in offsets]
    chip_offsets, chip_opposite, chip_hops = ordered(planes, z_n, x_n)
    chip_at = [(ctx_of(dy, dz), lax.rem(x + dx, x_n)) for dy, dz, dx in chip_offsets]
    cuts = chip_groups(planes, z_n, x_n)
    groups = [span(chip_hops, low, high) for low, high in cuts]
    group_at = [[low <= h <= high for low, high in cuts].index(True) for h in chip_hops]

    def send(src, dst, at_send, at_recv, device):
        pltpu.make_async_remote_copy(
            src_ref=src,
            dst_ref=dst,
            send_sem=at_send,
            recv_sem=at_recv,
            device_id=device,
            device_id_type=MESH,
        ).start()

    inputs = []
    for at, (src, dst) in enumerate(
        (
            (query_hbm, query),
            (draft_hbm, draft),
            (lengths_hbm, lengths),
            (residual_hbm, residual),
            (gain_hbm, gain),
        )
    ):
        copy = pltpu.make_async_copy(src, dst, input_sem.at[at])
        copy.start()
        inputs.append(copy)
    cache_copies = []
    for b in range(batch):
        copy = pltpu.make_async_copy(cache_hbm.at[:, b], cache.at[:, b], cache_sem.at[b])
        copy.start()
        cache_copies.append(copy)

    barrier = pltpu.get_barrier_semaphore()

    @pl.loop(1, ctx_n)
    def _(i):
        pl.semaphore_signal(
            barrier, inc=1, device_id=(lax.rem(ctx + i, ctx_n), kvh), device_id_type=MESH
        )

    @pl.loop(1, kvh_n)
    def _(i):
        pl.semaphore_signal(
            barrier, inc=1, device_id=(ctx, lax.rem(kvh + i, kvh_n)), device_id_type=MESH
        )

    for copy in inputs:
        copy.wait()

    for t in range(steps):
        row = query[t].astype(F32)
        for h in range(ctx_n):
            at = h * tokens + t * batch
            queries[at : at + batch, :] = row[:, h * LANES : (h + 1) * LANES]

    lane = lax.broadcasted_iota(jnp.int32, (ctx_n * steps, LANES), 1)
    position = ctx * shard_len + lax.broadcasted_iota(jnp.int32, (ctx_n * steps, shard_len), 1)
    draft_row = lax.broadcasted_iota(jnp.int32, (ctx_n * steps, tokens), 0)
    draft_col = lax.broadcasted_iota(jnp.int32, (ctx_n * steps, tokens), 1)
    draft_step = lax.div(draft_col, batch) + ctx * steps
    weight_copies = []
    for b in range(batch):
        cache_copies[b].wait()
        if b == batch - 1:
            for at, (src, dst) in enumerate(
                (
                    (out_hbm, out_w),
                    (gate_hbm, gate_up_w.at[0:units]),
                    (up_hbm, gate_up_w.at[units : 2 * units]),
                    (down_hbm, down_w),
                )
            ):
                copy = pltpu.make_async_copy(src, dst, weight_sem.at[at])
                copy.start()
                weight_copies.append(copy)
        mine = pl.ds(b, ctx_n * steps, stride=batch)
        q = queries[mine, :].astype(BF16)
        seen = position < lengths[b]
        scores = jnp.where(seen, dot_rows(q, cache[0, b]) * scale, HIDE)
        draft_seen = (draft_step <= lax.rem(draft_row, steps)) & (
            lax.rem(draft_col, batch) == b
        )
        draft_scores = jnp.where(draft_seen, dot_rows(q, draft[0]) * scale, HIDE)
        top = jnp.maximum(
            jnp.max(scores, axis=1, keepdims=True), jnp.max(draft_scores, axis=1, keepdims=True)
        )
        top = top.astype(BF16).astype(F32)
        weights = jnp.where(seen, jnp.exp(scores - top), 0.0)
        draft_weights = jnp.where(draft_seen, jnp.exp(draft_scores - top), 0.0)
        total = jnp.sum(weights, axis=1, keepdims=True) + jnp.sum(
            draft_weights, axis=1, keepdims=True
        )
        numer[mine, :] = dot(weights.astype(BF16), cache[1, b]) + dot(
            draft_weights.astype(BF16), draft[1]
        )
        stats[mine, :] = jnp.where(lane < 64, top, total)
    by_head = (ctx_n, tokens, LANES)
    att_msg[:, 0:tokens, :] = numer[...].reshape(by_head).astype(BF16)
    wide = stats[...].reshape(by_head)
    high = wide.astype(BF16).astype(F32)
    lanes3 = lax.broadcasted_iota(jnp.int32, by_head, 2)
    att_msg[:, tokens : 2 * tokens, :] = jnp.where(lanes3 < 96, high, wide - high).astype(BF16)

    pl.semaphore_wait(barrier, ctx_n + kvh_n - 2)

    for n in range(ctx_n - 1, 0, -1):
        to = ctx_at[n]
        send(
            att_msg.at[to],
            att_in.at[opposite[n]],
            send_sem.at[0],
            part_sem.at[0 if hops[n] <= 2 else 1],
            (to, kvh),
        )
    att_in[0] = att_msg[ctx]

    gains[kvh, ctx] = gain[...]

    @pl.loop(1, ctx_n)
    def _(i):
        to = lax.rem(ctx + i, ctx_n)
        send(gains.at[kvh, ctx], gains.at[kvh, ctx], send_sem.at[1], recv_sem.at[1], (to, kvh))

    def side(n, which):
        at_ctx, at_x = chip_at[n]
        return pl.ds(pl.multiple_of(((at_ctx * x_n + at_x) * 2 + which) * LANES, LANES), LANES)

    def hand_over(src, dst, at_send, at_recv):
        for n in range(chips):
            send(
                src.at[:, side(n, 1 - core)],
                dst.at[:, n * LANES : (n + 1) * LANES],
                at_send,
                at_recv,
                partner,
            )

    hand_over(gate_hbm, gate_up_other.at[0:units], send_sem.at[9], recv_sem.at[6])

    def merged(low, high):
        parts = [att_in[i, tokens : 2 * tokens, :].astype(F32) for i in range(low, high)]
        tops = [jnp.broadcast_to(p[:, 0:1], (tokens, LANES)) for p in parts]
        highest = functools.reduce(jnp.maximum, tops)
        factors = [jnp.exp(t - highest) for t in tops]
        denominator = sum(f * (p[:, 64:65] + p[:, 96:97]) for f, p in zip(factors, parts))
        numerator = sum(
            f * att_in[low + i, 0:tokens, :].astype(F32) for i, f in enumerate(factors)
        )
        return highest, denominator, numerator

    low, high = span(hops, 0, 2)
    drain(att_in.at[0 : high - 1], part_sem.at[0])
    highest, denominator, numerator = merged(low, high)
    if high < ctx_n:
        drain(att_in.at[high:ctx_n], part_sem.at[1])
        highest2, denominator2, numerator2 = merged(high, ctx_n)
        top = jnp.maximum(highest, highest2)
        factor, factor2 = jnp.exp(highest - top), jnp.exp(highest2 - top)
        denominator = factor * denominator + factor2 * denominator2
        numerator = factor * numerator + factor2 * numerator2
    heads[0] = (numerator / denominator).astype(BF16)

    for n in range(ctx_n - 1, 0, -1):
        send(
            heads.at[0],
            heads.at[opposite[n]],
            send_sem.at[2],
            head_sem.at[max(hops[n] - 1, 0)],
            (ctx_at[n], kvh),
        )

    hand_over(up_hbm, gate_up_other.at[units : 2 * units], send_sem.at[10], recv_sem.at[7])

    drain(gains.at[0, 0 : ctx_n - 1], recv_sem.at[1])

    @pl.loop(1, kvh_n)
    def _(i):
        to = lax.rem(kvh + i, kvh_n)
        send(gains.at[kvh], gains.at[kvh], send_sem.at[3], recv_sem.at[3], (ctx, to))

    weight_copies[0].wait()
    projected = jnp.zeros((tokens, kvh_n * LANES), F32)
    for at, (first, last) in enumerate(((0, 1), (2, 2), (3, hops[-1]))):
        if first > last:
            continue
        low, high = span(hops, first, last)
        for k in range(max(first, 1), last + 1):
            start, end = span(hops, k, k)
            drain(heads.at[start:end], head_sem.at[k - 1])
        attended = jnp.concatenate([heads[n] for n in range(low, high)], axis=1)
        rows = jnp.concatenate(
            [
                out_w[pl.ds(pl.multiple_of(ctx_at[n] * LANES, LANES), LANES), :]
                for n in range(low, high)
            ],
            axis=0,
        )
        projected = projected + dot(attended, rows)
    for k in range(kvh_n):
        proj_msg[k] = projected[:, k * LANES : (k + 1) * LANES].astype(BF16)

    @pl.loop(1, kvh_n)
    def _(i):
        to = lax.rem(kvh + i, kvh_n)
        send(proj_msg.at[to], proj_in.at[kvh], send_sem.at[4], recv_sem.at[4], (ctx, to))

    proj_in[kvh] = proj_msg[kvh]
    hand_over(down_hbm, down_other, send_sem.at[11], recv_sem.at[8])
    drain(gains.at[0 : kvh_n - 1], recv_sem.at[3])
    drain(proj_in.at[0 : kvh_n - 1], recv_sem.at[4])
    carried = residual[...].astype(F32)
    for k in range(kvh_n):
        carried = carried + proj_in[k].astype(F32)
    carried = carried.astype(BF16)
    feats[0] = carried

    for n in range(1, chips):
        to_ctx, to_x = chip_at[n]
        send(
            feats.at[0],
            feats.at[chip_opposite[n]],
            send_sem.at[5],
            feat_sem.at[group_at[n]],
            (to_ctx, to_x * 2 + core),
        )

    weight_copies[1].wait()
    weight_copies[2].wait()
    drain(gate_up_other.at[0:units], recv_sem.at[6])
    drain(gate_up_other.at[units : 2 * units], recv_sem.at[7])
    products = jnp.zeros((tokens, 2 * units), F32)
    products_other = jnp.zeros((tokens, 2 * units), F32)
    squares = jnp.zeros((tokens, LANES), F32)
    for g, (low, high) in enumerate(groups):
        drain(feats.at[low : high - 1 if g == 0 else high], feat_sem.at[g])
        pieces = []
        for n in range(low, high):
            at_ctx, at_x = chip_at[n]
            piece = feats[n].astype(F32)
            squares = squares + piece * piece
            pieces.append((piece * gains[at_x * 2 + core, at_ctx]).astype(BF16))
        rows = jnp.concatenate(pieces, axis=1)
        matching = jnp.concatenate([gate_up_w[:, side(n, core)] for n in range(low, high)], axis=1)
        products = products + dot_rows(rows, matching)
        matching = gate_up_other[:, low * LANES : high * LANES]
        products_other = products_other + dot_rows(rows, matching)
    halves_out[0] = products
    halves_out[1] = products_other
    squares_out[...] = squares
    send(halves_out, halves_in, send_sem.at[6], recv_sem.at[9], partner)
    send(squares_out, squares_in, send_sem.at[7], recv_sem.at[10], partner)
    drain(halves_in, recv_sem.at[9])
    drain(squares_in, recv_sem.at[10])
    squares = squares + squares_in[...]
    mean_square = jnp.sum(squares, axis=1, keepdims=True) / (chips * 2 * LANES)
    inverse = lax.rsqrt(mean_square + EPSILON)

    def activated(total):
        gate = total[:, 0:units] * inverse
        up = total[:, units : 2 * units] * inverse
        return (gate / (1.0 + jnp.exp(-gate)) * up).astype(BF16)

    hidden = activated(products + halves_in[1])
    hidden_other = activated(products_other + halves_in[0])

    weight_copies[3].wait()
    drain(down_other, recv_sem.at[8])
    for low, high in groups[:1:-1] + [(0, groups[1][1])]:
        matching = jnp.concatenate([down_w[:, side(n, core)] for n in range(low, high)], axis=1)
        block = dot(hidden, matching)
        block = block + dot(hidden_other, down_other[:, low * LANES : high * LANES])
        for n in range(high - 1, low - 1, -1):
            pair_msg[n] = block[:, (n - low) * LANES : (n - low + 1) * LANES].astype(BF16)
        for n in range(high - 1, max(low, 1) - 1, -1):
            to_ctx, to_x = chip_at[n]
            send(
                pair_msg.at[n],
                down_in.at[chip_opposite[n]],
                send_sem.at[8],
                recv_sem.at[5],
                (to_ctx, to_x * 2 + core),
            )
    down_in[0] = pair_msg[0]
    drain(down_in.at[0 : chips - 1], recv_sem.at[5])
    final = carried.astype(F32) + jnp.sum(down_in[...].astype(F32), axis=0)
    result[...] = final.astype(BF16)

    drain(att_in.at[0 : ctx_n - 1], send_sem.at[0])
    drain(gains.at[0, 0 : ctx_n - 1], send_sem.at[1])
    drain(heads.at[0 : ctx_n - 1], send_sem.at[2])
    drain(gains.at[0 : kvh_n - 1], send_sem.at[3])
    drain(proj_in.at[0 : kvh_n - 1], send_sem.at[4])
    drain(down_in.at[0 : chips - 1], send_sem.at[5])
    drain(halves_in, send_sem.at[6])
    drain(squares_in, send_sem.at[7])
    drain(down_in.at[0 : chips - 1], send_sem.at[8])
    drain(down_other, send_sem.at[9])
    drain(down_other, send_sem.at[10])
    drain(down_other, send_sem.at[11])


def per_device(ctx_n, kvh_n, planes, *arguments):
    (
        query,
        new_kv,
        kv_cache,
        lengths,
        residual,
        out_weight,
        norm_gain,
        gate_weight,
        up_weight,
        down_weight,
    ) = arguments
    steps, batch, query_width = query.shape
    heads = query_width // LANES
    assert heads == ctx_n and kv_cache.shape[2] == 1
    tokens = steps * batch
    chips = ctx_n * kvh_n // 2
    x_n = kvh_n // 2
    group_n = len(chip_groups(planes, ctx_n // planes, x_n))
    cache = kv_cache.reshape(2, batch, kv_cache.shape[3], LANES)
    units = gate_weight.shape[0]
    vmem = pl.BlockSpec(memory_space=pltpu.VMEM)
    far = pl.BlockSpec(memory_space=pl.ANY)
    dma = pltpu.SemaphoreType.DMA
    out = pl.pallas_call(
        functools.partial(layer_kernel, (ctx_n, kvh_n, planes, steps, batch)),
        out_shape=pltpu.VMEM((tokens, LANES), BF16),
        in_specs=[far] * 10,
        out_specs=vmem,
        scratch_shapes=[
            pltpu.VMEM(query.shape, BF16),
            pltpu.VMEM((2, tokens, LANES), BF16),
            pltpu.SMEM((batch,), jnp.int32),
            pltpu.VMEM((tokens, LANES), BF16),
            pltpu.VMEM((1, LANES), F32),
            pltpu.VMEM(cache.shape, BF16),
            pltpu.VMEM(out_weight.shape, BF16),
            pltpu.VMEM((2 * units, gate_weight.shape[1]), BF16),
            pltpu.VMEM(down_weight.shape, BF16),
            pltpu.VMEM((2 * units, chips * LANES), BF16),
            pltpu.VMEM((units, chips * LANES), BF16),
            pltpu.VMEM((ctx_n * tokens, LANES), F32),
            pltpu.VMEM((ctx_n * tokens, LANES), F32),
            pltpu.VMEM((ctx_n * tokens, LANES), F32),
            pltpu.VMEM((ctx_n, 2 * tokens, LANES), BF16),
            pltpu.VMEM((ctx_n, 2 * tokens, LANES), BF16),
            pltpu.VMEM((ctx_n, tokens, LANES), BF16),
            pltpu.VMEM((kvh_n, tokens, LANES), BF16),
            pltpu.VMEM((kvh_n, tokens, LANES), BF16),
            pltpu.VMEM((kvh_n, ctx_n, 1, LANES), F32),
            pltpu.VMEM((chips, tokens, LANES), BF16),
            pltpu.VMEM((2, tokens, 2 * units), F32),
            pltpu.VMEM((2, tokens, 2 * units), F32),
            pltpu.VMEM((tokens, LANES), F32),
            pltpu.VMEM((tokens, LANES), F32),
            pltpu.VMEM((chips, tokens, LANES), BF16),
            pltpu.VMEM((chips, tokens, LANES), BF16),
            dma((5,)),
            dma((batch,)),
            dma((4,)),
            dma((12,)),
            dma((11,)),
            dma((2,)),
            dma((planes // 2 + ctx_n // planes // 2,)),
            dma((group_n,)),
        ],
        compiler_params=pltpu.CompilerParams(
            collective_id=0, has_side_effects=True, vmem_limit_bytes=56 * 2**20
        ),
        name="layer",
    )(
        query,
        new_kv.reshape(2, tokens, LANES),
        lengths,
        residual.reshape(tokens, LANES),
        norm_gain.reshape(1, LANES),
        cache,
        out_weight,
        gate_weight,
        up_weight,
        down_weight,
    )
    return out.reshape(steps, batch, LANES)


def solution(mesh):
    ctx_n, kvh_n = mesh.shape["ctx"], mesh.shape["kvh"]
    planes = 4 if ctx_n % 4 == 0 and ctx_n > 4 else 2
    return jax.shard_map(
        functools.partial(per_device, ctx_n, kvh_n, planes),
        mesh=mesh,
        in_specs=(
            P(None, None, "kvh"),
            P(None, None, None, "kvh"),
            P(None, None, "kvh", "ctx", None),
            P(),
            P(None, None, ("ctx", "kvh")),
            P("kvh", "ctx"),
            P(("ctx", "kvh")),
            P(("ctx", "kvh"), None),
            P(("ctx", "kvh"), None),
            P(("ctx", "kvh"), None),
        ),
        out_specs=P(None, None, ("ctx", "kvh")),
        check_vma=False,
    )
```
